256 devices in a mesh: dp: 16 (over z, core), fsdp: 16 (over y, x).
Axes of the slice: x: 4, y: 4, z: 8, core: 2. Of those that a mesh axis runs over, the one named last changes fastest.
Arguments:
- hidden: bfloat16 [65536, 8192], P(('dp', 'fsdp')), may hold values from -8 to 8
- gain: float32 [8192], replicated, may hold values from 0.1 to 1.9
- qkv_weight: bfloat16 [8192, 1280], P('fsdp'), may hold values from -4 to 4
- owner_segment: int32 [65536], P(('dp', 'fsdp')), may hold values from 0 to 15, as said below
- target_row: int32 [65536], P(('dp', 'fsdp')), may hold values from 0 to 65535, as said below
Outputs:
- context: bfloat16 [65536, 1024], P(('dp', 'fsdp'))
The draws below stay inside these ranges and needn't reach their ends.
Inputs may be any that keep to these rules, and one draw needn't show every extreme that they name: `owner_segment`: rows of one device with equal values form one sequence, and the values never fall along a device's rows. `target_row`: A permutation of the rows. A row goes to a device of the same fsdp index; a sequence's rows land on consecutive rows of one device, in order; at most 32 rows of one device go to one device, and some device sends exactly 32 to one in every draw.
All inputs are finite; a program needn't handle non-finite values.
Results may differ from the reference program's by a relative error of at most 0.012.
The reference program's roundings to bfloat16 on the way count: a program that leaves them out, or rounds other values in their place, can miss the bound.
Values may be sent and summed in bfloat16 or wider, within the bound.
A program may use at most 128 MiB of HBM per device.

```python
import math
import jax
import jax.numpy as jnp
from jax import lax

D = 8192
HEAD = 128
GROUP = 8
TOK_DEV = 256
TOKENS = 65536
N_DP = 16
N_FSDP = 16


def balance_plan(key):
    shards = N_DP
    columns = N_FSDP
    middle = TOK_DEV // shards
    key_perm, key_size, key_order = jax.random.split(key, 3)
    perms = jax.vmap(lambda k: jax.random.permutation(k, shards))(jax.random.split(key_perm, columns))
    spread = jax.random.randint(key_size, (columns, shards // 2), 0, middle + 1)
    spread = spread.at[:, 0].set(middle)
    lengths = jnp.stack([middle + spread, middle - spread], axis=2).reshape(columns, shards)
    order = jax.vmap(lambda k: jax.random.permutation(k, shards))(jax.random.split(key_order, columns))
    lengths = jnp.take_along_axis(lengths, order, axis=1)
    target = jnp.arange(shards, dtype=jnp.int32)
    shift = (target[None, None, :] - perms[:, :, None]) % shards
    counts = jnp.take_along_axis(jnp.broadcast_to(lengths[:, None, :], (columns, shards, shards)), shift, axis=2)
    offset = jnp.cumsum(counts, axis=1) - counts
    finish = jnp.cumsum(counts, axis=2)
    begin = finish - counts
    rows = jnp.arange(TOK_DEV, dtype=jnp.int32)
    chosen = jnp.sum((finish[:, :, None, :] <= rows[None, None, :, None]).astype(jnp.int32), axis=3)
    first = jnp.take_along_axis(begin, chosen, axis=2)
    placed = jnp.take_along_axis(offset, chosen, axis=2)
    column = jnp.arange(columns, dtype=jnp.int32)[:, None, None]
    target_rows = (chosen * columns + column) * TOK_DEV + placed + rows[None, None, :] - first
    segments = jnp.transpose(chosen, (1, 0, 2)).reshape(-1).astype(jnp.int32)
    targets = jnp.transpose(target_rows, (1, 0, 2)).reshape(-1).astype(jnp.int32)
    return (segments, targets)


def draw_owner_segment(key, part):
    segments, targets = balance_plan(key)
    return segments


def draw_target_row(key, part):
    segments, targets = balance_plan(key)
    return targets


def draw_hidden(key, part):
    key = jax.random.fold_in(key, 3)
    key_base, key_scale = jax.random.split(key)
    base = jax.random.normal(key_base, (TOKENS, D), jnp.float32)
    scale = jnp.exp(jax.random.uniform(key_scale, (TOKENS, 1), jnp.float32, math.log(0.3), math.log(3.0)))
    rows = base * scale
    return jnp.clip(rows, -8.0, 8.0).astype(jnp.bfloat16)


def draw_qkv_weight(key, part):
    key = jax.random.fold_in(key, 5)
    key_base = jax.random.fold_in(key, 0)
    width = (GROUP + 2) * HEAD
    base = jax.random.normal(key_base, (D, width), jnp.float32) / math.sqrt(D)
    return jnp.clip(base, -4.0, 4.0).astype(jnp.bfloat16)


def setup_inputs(seed: int = 0) -> dict:
    key_list = jax.random.split(jax.random.key(seed), 6)
    return {
        "hidden": draw_hidden(jax.random.fold_in(key_list[5], 71), 0),
        "gain": jnp.clip(1.0 + 0.18 * jax.random.normal(key_list[1], (D,), jnp.float32), 0.1, 1.9),
        "qkv_weight": draw_qkv_weight(jax.random.fold_in(key_list[5], 71), 0),
        "owner_segment": draw_owner_segment(jax.random.fold_in(key_list[5], 71), 0),
        "target_row": draw_target_row(jax.random.fold_in(key_list[5], 71), 0),
    }


EPS = 1e-05

def attend(projected, segment, position):
    count = projected.shape[0]
    query = projected[:, :GROUP * HEAD].reshape(count, GROUP, HEAD).astype(jnp.float32)
    keys = projected[:, GROUP * HEAD:(GROUP + 1) * HEAD].astype(jnp.float32)
    values = projected[:, (GROUP + 1) * HEAD:].astype(jnp.float32)
    scores = jnp.einsum('qgh,kh->gqk', query, keys) * HEAD ** (-0.5)
    allowed = (segment[:, None] == segment[None, :]) & (position[None, :] <= position[:, None])
    scores = jnp.where(allowed[None], scores, -1e+30)
    peak = lax.optimization_barrier(jnp.max(scores, axis=2, keepdims=True))
    expos = jnp.exp(scores - peak)
    weights = (expos / lax.optimization_barrier(jnp.sum(expos, axis=2, keepdims=True))).astype(jnp.bfloat16)
    context = jnp.einsum('gqk,kh->qgh', weights.astype(jnp.float32), values)
    return context.reshape(count, GROUP * HEAD).astype(jnp.bfloat16)

def reference(hidden, gain, qkv_weight, owner_segment, target_row):
    blocks_all = TOKENS // TOK_DEV
    blocks = hidden.reshape(blocks_all, TOK_DEV, D)
    segments = owner_segment.reshape(blocks_all, TOK_DEV)
    position = jnp.arange(TOK_DEV, dtype=jnp.int32)

    def one_block(pair):
        rows, segment = pair
        values = rows.astype(jnp.float32)
        normed = (values * lax.rsqrt(lax.optimization_barrier(jnp.mean(values * values, axis=1, keepdims=True)) + EPS) * gain).astype(jnp.bfloat16)
        projected = jnp.dot(normed, qkv_weight, preferred_element_type=jnp.float32).astype(jnp.bfloat16)
        return attend(projected, segment, position)
    contexts = lax.map(one_block, (blocks, segments)).reshape(TOKENS, GROUP * HEAD)
    return jnp.zeros_like(contexts).at[target_row].set(contexts)
```

```python
import jax
import jax.numpy as jnp
from jax import lax
from jax.experimental import pallas as pl
from jax.experimental.pallas import tpu as pltpu
from jax.sharding import PartitionSpec as P

MESH = pl.DeviceIdType.MESH
HEAD = 128
EPS = 1e-05
ROWS = 256
FEATURES = 8192
PEERS = 16
CAPACITY = 32
WIDTH = 256
STARTS = (1024, 0, 256, 512, 768)
CHUNKS = len(STARTS)
QUERIES = CHUNKS - 1


def nt(a, b):
    return lax.dot_general(a, b, (((1,), (1,)), ((), ())), preferred_element_type=jnp.float32)


def nn(a, b):
    return jnp.dot(a, b, preferred_element_type=jnp.float32)


def kernel(
    hidden, gain, weight, segment, target, out,
    gathered, normed, total, keys, values, mask, spread, collect,
    outgoing, incoming, slots_out, slots_in,
    local_sem, g_send, g_recv, a_send, a_recv, s_send, s_recv,
):
    dp, fsdp = lax.axis_index("dp"), lax.axis_index("fsdp")
    core = lax.rem(dp, 2)
    y, x = fsdp // 4, lax.rem(fsdp, 4)
    x_up, x_down, x_far = lax.rem(x + 1, 4), lax.rem(x + 3, 4), lax.rem(x + 2, 4)
    y_up, y_down, y_far = lax.rem(y + 1, 4), lax.rem(y + 3, 4), lax.rem(y + 2, 4)
    to_x_up, to_x_down = (dp, y * 4 + x_up), (dp, y * 4 + x_down)
    to_y_up, to_y_down = (dp, y_up * 4 + x), (dp, y_down * 4 + x)
    sibling = (dp + 1 - 2 * core, fsdp)

    barrier = pltpu.get_barrier_semaphore()
    for neighbour in (to_x_up, to_x_down, to_y_up, to_y_down):
        pl.semaphore_signal(barrier, inc=1, device_id=neighbour, device_id_type=MESH)

    def greet(k, carry):
        peer = (lax.rem(dp + k, PEERS), fsdp)
        pl.semaphore_signal(barrier, inc=1, device_id=peer, device_id_type=MESH)
        return carry

    lax.fori_loop(1, PEERS, greet, 0)

    own = [
        pltpu.make_async_copy(
            weight.at[core, :, :, pl.ds(STARTS[j], WIDTH)],
            gathered.at[j, y, x, core],
            local_sem.at[j],
        )
        for j in range(CHUNKS)
    ]
    for copy in own:
        copy.start()
    load = pltpu.make_async_copy(hidden, normed, local_sem.at[CHUNKS])
    load.start()
    pl.semaphore_wait(barrier, 4 + PEERS - 1)

    def send(j, n, view, device):
        pltpu.make_async_remote_copy(
            src_ref=view, dst_ref=view, send_sem=g_send.at[j, n], recv_sem=g_recv.at[j, n],
            device_id=device, device_id_type=MESH,
        ).start()

    def landed(j, n, view):
        pltpu.make_async_remote_copy(
            src_ref=view, dst_ref=view, send_sem=g_send.at[j, n], recv_sem=g_recv.at[j, n],
            device_id=sibling, device_id_type=MESH,
        ).wait_recv()

    low, high = pl.ds(0, 64), pl.ds(64, 64)
    first, second = pl.ds(0, 2), pl.ds(2, 2)

    def own_blocks(j):
        own[j].wait()
        send(j, 0, gathered.at[j, y, x, core, 0], to_x_up)
        send(j, 1, gathered.at[j, y, x, core, 0], to_x_down)
        send(j, 2, gathered.at[j, y, x, core, 1], to_y_up)
        send(j, 3, gathered.at[j, y, x, core, 1], to_y_down)

    def pass_blocks(j):
        landed(j, 0, gathered.at[j, y, x_down, core, 0])
        send(j, 4, gathered.at[j, y, x_down, core, 0, low], to_x_up)
        landed(j, 1, gathered.at[j, y, x_up, core, 0])
        send(j, 5, gathered.at[j, y, x_up, core, 0, high], to_x_down)
        landed(j, 2, gathered.at[j, y_down, x, core, 1])
        send(j, 6, gathered.at[j, y_down, x, core, 1, low], to_y_up)
        landed(j, 3, gathered.at[j, y_up, x, core, 1])
        send(j, 7, gathered.at[j, y_up, x, core, 1, high], to_y_down)

    def own_lines(j):
        landed(j, 4, gathered.at[j, y, x_far, core, 0, low])
        landed(j, 5, gathered.at[j, y, x_far, core, 0, high])
        send(j, 8, gathered.at[j, y, :, core, 0], to_y_up)
        send(j, 9, gathered.at[j, y, :, core, 0], to_y_down)
        landed(j, 6, gathered.at[j, y_far, x, core, 1, low])
        landed(j, 7, gathered.at[j, y_far, x, core, 1, high])
        send(j, 10, gathered.at[j, :, x, core, 1], to_x_up)
        send(j, 11, gathered.at[j, :, x, core, 1], to_x_down)
        send(j, 16, gathered.at[j, y, :, core, 0], sibling)
        send(j, 20, gathered.at[j, :, x, core, 1], sibling)

    def pass_lines(j):
        landed(j, 8, gathered.at[j, y_down, :, core, 0])
        send(j, 12, gathered.at[j, y_down, first, core, 0], to_y_up)
        landed(j, 9, gathered.at[j, y_up, :, core, 0])
        send(j, 13, gathered.at[j, y_up, second, core, 0], to_y_down)
        landed(j, 10, gathered.at[j, :, x_down, core, 1])
        send(j, 14, gathered.at[j, first, x_down, core, 1], to_x_up)
        landed(j, 11, gathered.at[j, :, x_up, core, 1])
        send(j, 15, gathered.at[j, second, x_up, core, 1], to_x_down)
        send(j, 17, gathered.at[j, y_down, :, core, 0], sibling)
        send(j, 18, gathered.at[j, y_up, :, core, 0], sibling)
        send(j, 21, gathered.at[j, :, x_down, core, 1], sibling)
        send(j, 22, gathered.at[j, :, x_up, core, 1], sibling)

    def last_lines(j):
        landed(j, 12, gathered.at[j, y_far, first, core, 0])
        landed(j, 13, gathered.at[j, y_far, second, core, 0])
        send(j, 19, gathered.at[j, y_far, :, core, 0], sibling)
        landed(j, 14, gathered.at[j, first, x_far, core, 1])
        landed(j, 15, gathered.at[j, second, x_far, core, 1])
        send(j, 23, gathered.at[j, :, x_far, core, 1], sibling)

    def from_sibling(j):
        other = 1 - core
        for n, line in ((16, y), (17, y_down), (18, y_up), (19, y_far)):
            landed(j, n, gathered.at[j, line, :, other, 0])
        for n, line in ((20, x), (21, x_down), (22, x_up), (23, x_far)):
            landed(j, n, gathered.at[j, :, line, other, 1])

    def all_sent(j):
        for n, rows in ((0, 1), (1, 1), (2, 1), (3, 1)):
            view = gathered.at[j, y, x, core, 0]
            pltpu.make_async_copy(view, view, g_send.at[j, n]).wait()
        for n in (4, 5, 6, 7):
            view = gathered.at[j, y, x, core, 0, low]
            pltpu.make_async_copy(view, view, g_send.at[j, n]).wait()
        for n in (8, 9, 10, 11, 16, 17, 18, 19, 20, 21, 22, 23):
            view = gathered.at[j, y, :, core, 0]
            pltpu.make_async_copy(view, view, g_send.at[j, n]).wait()
        for n in (12, 13, 14, 15):
            view = gathered.at[j, y, first, core, 0]
            pltpu.make_async_copy(view, view, g_send.at[j, n]).wait()

    def plan():
        goal = target[...]
        shard, slot = goal >> 12, goal & (ROWS - 1)
        chosen = lax.broadcasted_iota(jnp.int32, (PEERS, ROWS), 0) == shard
        onehot = chosen.astype(jnp.float32)
        earlier = (
            lax.broadcasted_iota(jnp.int32, (ROWS, ROWS), 0)
            < lax.broadcasted_iota(jnp.int32, (ROWS, ROWS), 1)
        ).astype(jnp.bfloat16)
        before = nn(onehot.astype(jnp.bfloat16), earlier)
        rank = jnp.sum(onehot * before, axis=0, keepdims=True).astype(jnp.int32)
        bucket = shard * CAPACITY + rank
        spread[...] = (
            lax.broadcasted_iota(jnp.int32, (PEERS * CAPACITY, ROWS), 0) == bucket
        ).astype(jnp.bfloat16)
        lane = rank + CAPACITY * lax.rem(dp, 4)
        place = (lax.broadcasted_iota(jnp.int32, (128, ROWS), 0) == lane).astype(jnp.bfloat16)
        marks = (onehot * (slot + 1).astype(jnp.float32)).astype(jnp.bfloat16)
        table = nt(marks, place)
        slots_out[...] = jnp.broadcast_to(table[:, None, :], (PEERS, 8, 128))

        def ship(k, carry):
            peer = lax.rem(dp + k, PEERS)
            pltpu.make_async_remote_copy(
                src_ref=slots_out.at[peer], dst_ref=slots_in.at[dp],
                send_sem=s_send.at[k], recv_sem=s_recv.at[k],
                device_id=(peer, fsdp), device_id_type=MESH,
            ).start()
            return carry

        lax.fori_loop(1, PEERS, ship, 0)
        slots_in[dp] = slots_out[dp]

        ids = jnp.broadcast_to(segment[...].astype(jnp.float32), (ROWS, ROWS))
        causal = lax.broadcasted_iota(jnp.int32, (ROWS, ROWS), 1) <= lax.broadcasted_iota(
            jnp.int32, (ROWS, ROWS), 0
        )
        mask[...] = ((ids == ids.T) & causal).astype(jnp.float32)

    def plan_arrivals():
        def wait(k, carry):
            source = lax.rem(dp + PEERS - k, PEERS)
            copy = pltpu.make_async_remote_copy(
                src_ref=slots_out.at[source], dst_ref=slots_in.at[source],
                send_sem=s_send.at[k], recv_sem=s_recv.at[k],
                device_id=(source, fsdp), device_id_type=MESH,
            )
            copy.wait_recv()
            copy.wait_send()
            return carry

        lax.fori_loop(1, PEERS, wait, 0)
        wanted = lax.broadcasted_iota(jnp.int32, (ROWS, 128), 0) + 1
        for t in range(4):
            row = slots_in[4 * t] + slots_in[4 * t + 1] + slots_in[4 * t + 2] + slots_in[4 * t + 3]
            row = row[0:1].astype(jnp.int32)
            collect[:, t * 128 : (t + 1) * 128] = (wanted == row).astype(jnp.bfloat16)

    def normalise():
        load.wait()

        def some(i, carry):
            rows = pl.ds(pl.multiple_of(i * 16, 16), 16)
            floats = normed[rows, :].astype(jnp.float32)
            scale = lax.rsqrt(jnp.mean(floats * floats, axis=1, keepdims=True) + EPS)
            normed[rows, :] = (floats * scale * gain[...]).astype(jnp.bfloat16)
            return carry

        lax.fori_loop(0, ROWS // 16, some, 0)

    def project(j):
        total[...] = jnp.zeros_like(total)

        def some(i, carry):
            columns = pl.ds(pl.multiple_of(i * 2048, 2048), 2048)
            block = gathered[j, i].reshape(2048, WIDTH)
            total[...] += nn(normed[:, columns], block)
            return carry

        lax.fori_loop(0, 4, some, 0)

    def attend(j):
        n = j - 1
        contexts = []
        for h in range(2):
            query = total[:, h * HEAD : (h + 1) * HEAD].astype(jnp.bfloat16)
            scores = nt(query, keys[...]) * HEAD ** (-0.5)
            scores = jnp.where(mask[...] > 0.5, scores, -1e30)
            expos = jnp.exp(scores - jnp.max(scores, axis=1, keepdims=True))
            weights = (expos / jnp.sum(expos, axis=1, keepdims=True)).astype(jnp.bfloat16)
            contexts.append(nn(weights, values[...]).astype(jnp.bfloat16))
        context = jnp.concatenate(contexts, axis=1)
        outgoing[n] = nn(spread[...], context).astype(jnp.bfloat16).reshape(PEERS, CAPACITY, WIDTH)

        def ship(k, carry):
            peer = lax.rem(dp + k, PEERS)
            pltpu.make_async_remote_copy(
                src_ref=outgoing.at[n, peer], dst_ref=incoming.at[n, dp],
                send_sem=a_send.at[n, k], recv_sem=a_recv.at[n, k],
                device_id=(peer, fsdp), device_id_type=MESH,
            ).start()
            return carry

        lax.fori_loop(1, PEERS, ship, 0)
        incoming[n, dp] = outgoing[n, dp]

    def deliver(j):
        n = j - 1

        def wait(k, carry):
            source = lax.rem(dp + PEERS - k, PEERS)
            copy = pltpu.make_async_remote_copy(
                src_ref=outgoing.at[n, source], dst_ref=incoming.at[n, source],
                send_sem=a_send.at[n, k], recv_sem=a_recv.at[n, k],
                device_id=(source, fsdp), device_id_type=MESH,
            )
            copy.wait_recv()
            copy.wait_send()
            return carry

        lax.fori_loop(1, PEERS, wait, 0)
        rows = incoming[n].reshape(PEERS * CAPACITY, WIDTH)
        out[:, n * WIDTH : (n + 1) * WIDTH] = nn(collect[...], rows).astype(jnp.bfloat16)

    def compute(j):
        from_sibling(j)
        project(j)
        if j == 0:
            keys[...] = total[:, :HEAD].astype(jnp.bfloat16)
            values[...] = total[:, HEAD:].astype(jnp.bfloat16)
        else:
            attend(j)

    own_blocks(0)
    own_blocks(1)
    plan()
    pass_blocks(0)
    own_lines(0)
    for j in range(CHUNKS):
        if j + 1 < CHUNKS:
            pass_blocks(j + 1)
        if j == 0:
            normalise()
        if j + 1 < CHUNKS:
            own_lines(j + 1)
        if j + 2 < CHUNKS:
            own_blocks(j + 2)
        pass_lines(j)
        if j == 0:
            plan_arrivals()
        if j >= 1:
            compute(j - 1)
        last_lines(j)
    compute(CHUNKS - 1)
    for j in range(1, CHUNKS):
        deliver(j)
    for j in range(CHUNKS):
        all_sent(j)


def per_device(hidden, gain, qkv_weight, owner_segment, target_row):
    any_space = pl.BlockSpec(memory_space=pl.ANY)
    vmem = pl.BlockSpec(memory_space=pltpu.VMEM)
    bf16, f32 = jnp.bfloat16, jnp.float32
    dma = pltpu.SemaphoreType.DMA
    return pl.pallas_call(
        kernel,
        out_shape=jax.ShapeDtypeStruct((ROWS, QUERIES * WIDTH), bf16),
        in_specs=[any_space, vmem, any_space, vmem, vmem],
        out_specs=vmem,
        scratch_shapes=[
            pltpu.VMEM((CHUNKS, 4, 4, 2, 2, 128, WIDTH), bf16),
            pltpu.VMEM((ROWS, FEATURES), bf16),
            pltpu.VMEM((ROWS, WIDTH), f32),
            pltpu.VMEM((ROWS, HEAD), bf16),
            pltpu.VMEM((ROWS, HEAD), bf16),
            pltpu.VMEM((ROWS, ROWS), f32),
            pltpu.VMEM((PEERS * CAPACITY, ROWS), bf16),
            pltpu.VMEM((ROWS, PEERS * CAPACITY), bf16),
            pltpu.VMEM((QUERIES, PEERS, CAPACITY, WIDTH), bf16),
            pltpu.VMEM((QUERIES, PEERS, CAPACITY, WIDTH), bf16),
            pltpu.VMEM((PEERS, 8, 128), f32),
            pltpu.VMEM((PEERS, 8, 128), f32),
            dma((CHUNKS + 1,)),
            dma((CHUNKS, 24)),
            dma((CHUNKS, 24)),
            dma((QUERIES, PEERS)),
            dma((QUERIES, PEERS)),
            dma((PEERS,)),
            dma((PEERS,)),
        ],
        compiler_params=pltpu.CompilerParams(
            collective_id=0, has_side_effects=True, vmem_limit_bytes=56 << 20
        ),
        cost_estimate=pl.CostEstimate(
            flops=2 * ROWS * FEATURES * 1280, bytes_accessed=6 << 20, transcendentals=8 * ROWS * ROWS
        ),
    )(
        hidden,
        gain.reshape(1, FEATURES),
        qkv_weight.reshape(2, 2, 128, 1280),
        owner_segment.reshape(1, ROWS),
        target_row.reshape(1, ROWS),
    )


def solution(mesh):
    in_specs = (P(("dp", "fsdp"), None), P(), P("fsdp", None), P(("dp", "fsdp")), P(("dp", "fsdp")))
    out_specs = P(("dp", "fsdp"), None)
    return jax.shard_map(
        per_device, mesh=mesh, in_specs=in_specs, out_specs=out_specs, check_vma=False
    )
```

```python
import jax
import jax.numpy as jnp
from jax import lax
from jax.experimental import pallas as pl
from jax.experimental.pallas import tpu as pltpu
from jax.sharding import PartitionSpec as P

MESH = pl.DeviceIdType.MESH
HEAD = 128
EPS = 1e-05
ROWS = 256
FEATURES = 8192
PEERS = 16
CAPACITY = 32
CHUNKS = ((1024, 256), (0, 256), (512, 256), (768, 128), (896, 128))
RING = (256, 256)
COLUMNS = 1024
NEAR, FAR, LINE, LAST, TWIN, TWIN_LAST = range(6)


def nt(a, b):
    return lax.dot_general(a, b, (((1,), (1,)), ((), ())), preferred_element_type=jnp.float32)


def nn(a, b):
    return jnp.dot(a, b, preferred_element_type=jnp.float32)


def kernel(
    hidden, gain, weight, segment, target, out,
    wide, narrow, ring, raw, normed, total, keys, values, mask, spread, collect,
    out_wide, in_wide, out_narrow, in_narrow, slots_out, slots_in,
    local_sem, g_send, g_recv, z_send, z_recv, a_send, a_recv, s_sem,
):
    dp, fsdp = lax.axis_index("dp"), lax.axis_index("fsdp")
    z, core = dp // 2, lax.rem(dp, 2)
    y, x = fsdp // 4, lax.rem(fsdp, 4)
    other = 1 - core
    x_up, x_down, x_far = lax.rem(x + 1, 4), lax.rem(x + 3, 4), lax.rem(x + 2, 4)
    y_up, y_down, y_far = lax.rem(y + 1, 4), lax.rem(y + 3, 4), lax.rem(y + 2, 4)
    to_x_up, to_x_down = (dp, y * 4 + x_up), (dp, y * 4 + x_down)
    to_y_up, to_y_down = (dp, y_up * 4 + x), (dp, y_down * 4 + x)
    to_z_up = (lax.rem(z + 1, 8) * 2 + core, fsdp)
    to_z_down = (lax.rem(z + 7, 8) * 2 + core, fsdp)
    sibling = (dp + other - core, fsdp)

    def chunk(j):
        return wide.at[j] if j < 3 else narrow.at[j - 3]

    barrier = pltpu.get_barrier_semaphore()

    def greet(k, carry):
        for peer in ((lax.rem(dp + k, PEERS), fsdp), (dp, lax.rem(fsdp + k, PEERS))):
            pl.semaphore_signal(barrier, inc=1, device_id=peer, device_id_type=MESH)
        return carry

    lax.fori_loop(1, PEERS, greet, 0)

    load = pltpu.make_async_copy(hidden, raw, local_sem.at[0])
    load.start()
    ring_half, ring_part = z // 4, lax.rem(z, 4)
    ring_place = (1 - ring_half) * (y * 4 + x) + ring_half * (x * 4 + y)
    own_ring = pltpu.make_async_copy(
        weight.at[core, ring_half, ring_part, :, pl.ds(*RING)],
        ring.at[ring_half, core, ring_place, ring_part],
        local_sem.at[1],
    )
    own_ring.start()
    own = []
    for j, (start, width) in enumerate(CHUNKS):
        for half, (line, place) in enumerate(((y, x), (x, y))):
            copy = pltpu.make_async_copy(
                weight.at[core, half, :, :, pl.ds(start, width)],
                chunk(j).at[half, core, line, place],
                local_sem.at[2 + 2 * j + half],
            )
            copy.start()
            own.append(copy)

    def send(view, device, send_sem, recv_sem):
        pltpu.make_async_remote_copy(
            src_ref=view, dst_ref=view, send_sem=send_sem, recv_sem=recv_sem,
            device_id=device, device_id_type=MESH,
        ).start()

    def landed(view, sem):
        pltpu.make_async_copy(view, view, sem).wait()

    low, high = pl.ds(0, 2), pl.ds(2, 2)

    def near(j):
        g, s, r = chunk(j), g_send.at[j], g_recv.at[j, NEAR]
        own[2 * j].wait()
        own[2 * j + 1].wait()
        send(g.at[0, core, y, x], to_x_up, s, r)
        send(g.at[0, core, y, x], to_x_down, s, r)
        send(g.at[1, core, x, y], to_y_up, s, r)
        send(g.at[1, core, x, y], to_y_down, s, r)

    def far(j):
        g, s, r = chunk(j), g_send.at[j], g_recv.at[j, FAR]
        landed(g.at[0, core, y], g_recv.at[j, NEAR])
        send(g.at[0, core, y, x_down, low], to_x_up, s, r)
        send(g.at[0, core, y, x_up, high], to_x_down, s, r)
        send(g.at[1, core, x, y_down, low], to_y_up, s, r)
        send(g.at[1, core, x, y_up, high], to_y_down, s, r)

    def lines(j):
        g, s, r, t = chunk(j), g_send.at[j], g_recv.at[j, LINE], g_recv.at[j, TWIN]
        landed(g.at[0, core, y, low], g_recv.at[j, FAR])
        send(g.at[0, core, y], to_y_up, s, r)
        send(g.at[0, core, y], to_y_down, s, r)
        send(g.at[1, core, x], to_x_up, s, r)
        send(g.at[1, core, x], to_x_down, s, r)
        send(g.at[0, core, y], sibling, s, t)
        send(g.at[1, core, x], sibling, s, t)

    def pass_lines(j):
        g, s, r, t = chunk(j), g_send.at[j], g_recv.at[j, LAST], g_recv.at[j, TWIN]
        landed(g.at[0, core], g_recv.at[j, LINE])
        send(g.at[0, core, y_down, low], to_y_up, s, r)
        send(g.at[0, core, y_up, high], to_y_down, s, r)
        send(g.at[1, core, x_down, low], to_x_up, s, r)
        send(g.at[1, core, x_up, high], to_x_down, s, r)
        send(g.at[0, core, y_down], sibling, s, t)
        send(g.at[0, core, y_up], sibling, s, t)
        send(g.at[1, core, x_down], sibling, s, t)
        send(g.at[1, core, x_up], sibling, s, t)

    def last_lines(j):
        g, s, t = chunk(j), g_send.at[j], g_recv.at[j, TWIN_LAST]
        landed(g.at[0, core, low], g_recv.at[j, LAST])
        send(g.at[0, core, y_far], sibling, s, t)
        send(g.at[1, core, x_far], sibling, s, t)

    def twin(j):
        landed(chunk(j).at[:, other, pl.ds(0, 3)], g_recv.at[j, TWIN])

    def twin_last(j):
        landed(chunk(j).at[:, other, 0], g_recv.at[j, TWIN_LAST])

    def ring_at(where, places=None):
        place = slice(None) if places is None else places
        return ring.at[where // 4, core, place, lax.rem(where, 4)]

    halves = (pl.ds(0, 8), pl.ds(8, 8))

    def z_up(n):
        return lax.rem(z + n, 8)

    def z_down(n):
        return lax.rem(z + 8 - n, 8)

    def plane():
        own_ring.wait()
        view = ring.at[ring_half, core, ring_place, ring_part]

        def ship(k, carry):
            send(view, (dp, lax.rem(fsdp + k, PEERS)), z_send.at[0], z_recv.at[0])
            return carry

        lax.fori_loop(1, PEERS, ship, 0)

    def ring_start():
        landed(ring_at(z, pl.ds(0, 15)), z_recv.at[0])
        for h in range(2):
            send(ring_at(z, halves[h]), to_z_up, z_send.at[1], z_recv.at[2 + h])
            send(ring_at(z, halves[h]), to_z_down, z_send.at[1], z_recv.at[2 + h])
        send(ring_at(z), sibling, z_send.at[1], z_recv.at[1])

    def ring_step(n, h):
        landed(ring_at(z), z_recv.at[2 * n + h])
        sem = z_recv.at[2 * n + 2 + h]
        if n < 3 or h == 0:
            send(ring_at(z_down(n), halves[h]), to_z_up, z_send.at[1], sem if n < 3 else z_recv.at[8])
        if n < 3 or h == 1:
            send(ring_at(z_up(n), halves[h]), to_z_down, z_send.at[1], sem if n < 3 else z_recv.at[8])
        if h == 1:
            send(ring_at(z_down(n)), sibling, z_send.at[1], z_recv.at[1])
            send(ring_at(z_up(n)), sibling, z_send.at[1], z_recv.at[1])

    def ring_end():
        landed(ring_at(z), z_recv.at[8])
        send(ring_at(z_up(4)), sibling, z_send.at[1], z_recv.at[1])

    def ring_twin():
        landed(ring.at[:, other], z_recv.at[1])

    def plan():
        goal = target[...]
        shard, slot = goal >> 12, goal & (ROWS - 1)
        chosen = lax.broadcasted_iota(jnp.int32, (PEERS, ROWS), 0) == shard
        onehot = chosen.astype(jnp.float32)
        earlier = (
            lax.broadcasted_iota(jnp.int32, (ROWS, ROWS), 0)
            < lax.broadcasted_iota(jnp.int32, (ROWS, ROWS), 1)
        ).astype(jnp.bfloat16)
        before = nn(onehot.astype(jnp.bfloat16), earlier)
        rank = jnp.sum(onehot * before, axis=0, keepdims=True).astype(jnp.int32)
        bucket = shard * CAPACITY + rank
        spread[...] = (
            lax.broadcasted_iota(jnp.int32, (PEERS * CAPACITY, ROWS), 0) == bucket
        ).astype(jnp.bfloat16)
        lane = rank + CAPACITY * lax.rem(dp, 4)
        place = (lax.broadcasted_iota(jnp.int32, (128, ROWS), 0) == lane).astype(jnp.bfloat16)
        marks = (onehot * (slot + 1).astype(jnp.float32)).astype(jnp.bfloat16)
        table = nt(marks, place)
        slots_out[...] = jnp.broadcast_to(table[:, None, :], (PEERS, 8, 128))
        ids = jnp.broadcast_to(segment[...].astype(jnp.float32), (ROWS, ROWS))
        causal = lax.broadcasted_iota(jnp.int32, (ROWS, ROWS), 1) <= lax.broadcasted_iota(
            jnp.int32, (ROWS, ROWS), 0
        )
        mask[...] = ((ids == ids.T) & causal).astype(jnp.float32)

    def to_peers(source, landing, send_sem, recv_sem):
        def ship(k, carry):
            peer = lax.rem(dp + k, PEERS)
            pltpu.make_async_remote_copy(
                src_ref=source.at[peer], dst_ref=landing.at[dp],
                send_sem=send_sem, recv_sem=recv_sem,
                device_id=(peer, fsdp), device_id_type=MESH,
            ).start()
            return carry

        lax.fori_loop(1, PEERS, ship, 0)
        landing[dp] = source[dp]

    def from_peers(landing, recv_sem):
        landed(landing.at[pl.ds(0, PEERS - 1)], recv_sem)

    def plan_arrivals():
        from_peers(slots_in, s_sem.at[1])
        wanted = lax.broadcasted_iota(jnp.int32, (ROWS, 128), 0) + 1
        for t in range(4):
            row = slots_in[4 * t] + slots_in[4 * t + 1] + slots_in[4 * t + 2] + slots_in[4 * t + 3]
            row = row[0:1].astype(jnp.int32)
            collect[:, t * 128 : (t + 1) * 128] = (wanted == row).astype(jnp.bfloat16)

    def normalise():
        def some(i, carry):
            rows = pl.ds(pl.multiple_of(i * 16, 16), 16)
            floats = raw[rows, :].astype(jnp.float32)
            scale = lax.rsqrt(jnp.mean(floats * floats, axis=1, keepdims=True) + EPS)
            for shard in range(16):
                for c in range(2):
                    for half in range(2):
                        a = shard * 512 + c * 256 + half * 128
                        at = (1 - half) * shard + half * (shard % 4 * 4 + shard // 4)
                        b = ((half * 2 + c) * 16 + at) * 128
                        part = raw[rows, a : a + 128].astype(jnp.float32)
                        normed[rows, b : b + 128] = (part * scale * gain[:, a : a + 128]).astype(
                            jnp.bfloat16
                        )
            return carry

        lax.fori_loop(0, ROWS // 16, some, 0)

    def project(g, width):
        total[:, :width] = jnp.zeros((ROWS, width), jnp.float32)

        def some(i, carry):
            columns = pl.ds(pl.multiple_of(i * 2048, 2048), 2048)
            block = g[i // 2, lax.rem(i, 2)].reshape(2048, width)
            total[:, :width] += nn(normed[:, columns], block)
            return carry

        lax.fori_loop(0, 4, some, 0)

    def project_lines(j, mine, width):
        g = chunk(j)
        sums = jnp.zeros((ROWS, width), jnp.float32)
        for half in range(2):
            for c in range(2):
                for line in mine[half]:
                    first = ((half * 2 + c) * 16 + line * 4) * 128
                    columns = pl.ds(pl.multiple_of(first, 512), 512)
                    sums = sums + nn(normed[:, columns], g[half, c, line].reshape(512, width))
        return sums

    def project_first(j, width):
        total[:, :width] = project_lines(j, ((y, y_up, y_down), (x, x_up, x_down)), width)

    def project_last(j, width):
        total[:, :width] += project_lines(j, ((y_far,), (x_far,)), width)

    def group(n):
        if n < 3:
            return out_wide.at[n], in_wide.at[n], 256, (RING[0], 0, 512)[n]
        return out_narrow.at[n - 3], in_narrow.at[n - 3], 128, (768, 896)[n - 3]

    def attend(n):
        outgoing, incoming, width, start = group(n)
        contexts = []
        for h in range(width // HEAD):
            query = total[:, h * HEAD : (h + 1) * HEAD].astype(jnp.bfloat16)
            scores = nt(query, keys[...]) * HEAD ** (-0.5)
            scores = jnp.where(mask[...] > 0.5, scores, -1e30)
            expos = jnp.exp(scores - jnp.max(scores, axis=1, keepdims=True))
            weights = (expos / jnp.sum(expos, axis=1, keepdims=True)).astype(jnp.bfloat16)
            contexts.append(nn(weights, values[...]).astype(jnp.bfloat16))
        context = jnp.concatenate(contexts, axis=1) if len(contexts) > 1 else contexts[0]
        outgoing[...] = nn(spread[...], context).astype(jnp.bfloat16).reshape(PEERS, CAPACITY, width)
        to_peers(outgoing, incoming, a_send.at[n], a_recv.at[n])

    def deliver(n):
        outgoing, incoming, width, start = group(n)
        from_peers(incoming, a_recv.at[n])
        rows = incoming[...].reshape(PEERS * CAPACITY, width)
        out[:, start : start + width] = nn(collect[...], rows).astype(jnp.bfloat16)

    plan()
    load.wait()
    normalise()
    pl.semaphore_wait(barrier, 2 * (PEERS - 1))

    plane()
    near(0)
    near(1)
    near(2)
    to_peers(slots_out, slots_in, s_sem.at[0], s_sem.at[1])
    ring_start()
    far(0)
    near(3)
    near(4)
    far(1)
    far(2)
    lines(0)
    far(3)
    far(4)
    ring_step(1, 0)
    lines(1)
    ring_step(1, 1)
    plan_arrivals()
    ring_step(2, 0)
    pass_lines(0)
    lines(2)
    ring_step(2, 1)
    ring_step(3, 0)
    pass_lines(1)
    ring_step(3, 1)
    last_lines(0)
    lines(3)
    twin(0)
    twin_last(0)
    project(chunk(0), 256)
    keys[...] = total[:, :HEAD].astype(jnp.bfloat16)
    values[...] = total[:, HEAD:].astype(jnp.bfloat16)
    ring_end()
    ring_twin()
    project(ring, 256)
    pass_lines(2)
    lines(4)
    attend(0)
    last_lines(1)
    twin(1)
    twin_last(1)
    project(chunk(1), 256)
    pass_lines(3)
    attend(1)
    last_lines(2)
    twin(2)
    twin_last(2)
    project(chunk(2), 256)
    pass_lines(4)
    attend(2)
    twin(3)
    project_first(3, 128)
    last_lines(3)
    twin_last(3)
    project_last(3, 128)
    attend(3)
    twin(4)
    project_first(4, 128)
    last_lines(4)
    twin_last(4)
    project_last(4, 128)
    attend(4)
    for n in range(5):
        deliver(n)
    for j, (start, width) in enumerate(CHUNKS):
        landed(raw.at[pl.ds(0, width), pl.ds(0, 7936)], g_send.at[j])
    landed(raw.at[pl.ds(0, 16), pl.ds(0, 7680)], z_send.at[0])
    landed(raw.at[pl.ds(0, 240)], z_send.at[1])
    landed(slots_out.at[pl.ds(0, PEERS - 1)], s_sem.at[0])
    for n in range(5):
        landed(group(n)[0].at[pl.ds(0, PEERS - 1)], a_send.at[n])


def per_device(hidden, gain, qkv_weight, owner_segment, target_row):
    any_space = pl.BlockSpec(memory_space=pl.ANY)
    vmem = pl.BlockSpec(memory_space=pltpu.VMEM)
    bf16, f32 = jnp.bfloat16, jnp.float32
    dma = pltpu.SemaphoreType.DMA
    return pl.pallas_call(
        kernel,
        out_shape=jax.ShapeDtypeStruct((ROWS, COLUMNS), bf16),
        in_specs=[any_space, vmem, any_space, vmem, vmem],
        out_specs=vmem,
        scratch_shapes=[
            pltpu.VMEM((3, 2, 2, 4, 4, 4, 32, 256), bf16),
            pltpu.VMEM((2, 2, 2, 4, 4, 4, 32, 128), bf16),
            pltpu.VMEM((2, 2, 16, 4, 32, 256), bf16),
            pltpu.VMEM((ROWS, FEATURES), bf16),
            pltpu.VMEM((ROWS, FEATURES), bf16),
            pltpu.VMEM((ROWS, 256), f32),
            pltpu.VMEM((ROWS, HEAD), bf16),
            pltpu.VMEM((ROWS, HEAD), bf16),
            pltpu.VMEM((ROWS, ROWS), f32),
            pltpu.VMEM((PEERS * CAPACITY, ROWS), bf16),
            pltpu.VMEM((ROWS, PEERS * CAPACITY), bf16),
            pltpu.VMEM((3, PEERS, CAPACITY, 256), bf16),
            pltpu.VMEM((3, PEERS, CAPACITY, 256), bf16),
            pltpu.VMEM((2, PEERS, CAPACITY, 128), bf16),
            pltpu.VMEM((2, PEERS, CAPACITY, 128), bf16),
            pltpu.VMEM((PEERS, 8, 128), f32),
            pltpu.VMEM((PEERS, 8, 128), f32),
            dma((2 + 2 * len(CHUNKS),)),
            dma((len(CHUNKS),)),
            dma((len(CHUNKS), 6)),
            dma((2,)),
            dma((9,)),
            dma((5,)),
            dma((5,)),
            dma((2,)),
        ],
        compiler_params=pltpu.CompilerParams(
            collective_id=0, has_side_effects=True, vmem_limit_bytes=56 << 20
        ),
        cost_estimate=pl.CostEstimate(
            flops=2 * ROWS * FEATURES * 1280, bytes_accessed=6 << 20, transcendentals=8 * ROWS * ROWS
        ),
    )(
        hidden,
        gain.reshape(1, FEATURES),
        qkv_weight.reshape(2, 2, 4, 32, 1280),
        owner_segment.reshape(1, ROWS),
        target_row.reshape(1, ROWS),
    )


def solution(mesh):
    in_specs = (P(("dp", "fsdp"), None), P(), P("fsdp", None), P(("dp", "fsdp")), P(("dp", "fsdp")))
    out_specs = P(("dp", "fsdp"), None)
    return jax.shard_map(
        per_device, mesh=mesh, in_specs=in_specs, out_specs=out_specs, check_vma=False
    )
```

```python
import jax
import jax.numpy as jnp
from jax import lax
from jax.experimental import pallas as pl
from jax.experimental.pallas import tpu as pltpu
from jax.sharding import PartitionSpec as P

MESH = pl.DeviceIdType.MESH
HEAD = 128
EPS = 1e-05
ROWS = 256
FEATURES = 8192
PEERS = 16
CAPACITY = 32
CHUNKS = ((1024, 256), (0, 256), (512, 256), (768, 128), (896, 128))
RING = (256, 256)
COLUMNS = 1024
DIRECT = (0, 1, 3, 4)
NEAR, FAR, LINE, LAST, TWIN, TWIN_LAST = range(6)


def nt(a, b):
    return lax.dot_general(a, b, (((1,), (1,)), ((), ())), preferred_element_type=jnp.float32)


def nn(a, b):
    return jnp.dot(a, b, preferred_element_type=jnp.float32)


def kernel(
    hidden, gain_in, weight, segment_in, target_in, out,
    wide, narrow, ring, raw, normed, gain, segment, target, total, keys, values, mask, spread, collect,
    out_wide, in_wide, out_narrow, in_narrow, slots_out, slots_in,
    local_sem, g_send, g_recv, z_send, z_recv, a_send, a_recv, s_sem,
):
    dp, fsdp = lax.axis_index("dp"), lax.axis_index("fsdp")
    z, core = dp // 2, lax.rem(dp, 2)
    y, x = fsdp // 4, lax.rem(fsdp, 4)
    other = 1 - core
    x_up, x_down, x_far = lax.rem(x + 1, 4), lax.rem(x + 3, 4), lax.rem(x + 2, 4)
    y_up, y_down, y_far = lax.rem(y + 1, 4), lax.rem(y + 3, 4), lax.rem(y + 2, 4)
    to_x_up, to_x_down = (dp, y * 4 + x_up), (dp, y * 4 + x_down)
    to_y_up, to_y_down = (dp, y_up * 4 + x), (dp, y_down * 4 + x)
    to_z_up = (lax.rem(z + 1, 8) * 2 + core, fsdp)
    to_z_down = (lax.rem(z + 7, 8) * 2 + core, fsdp)
    sibling = (dp + other - core, fsdp)

    def chunk(j):
        return wide.at[j] if j < 3 else narrow.at[j - 3]

    barrier = pltpu.get_barrier_semaphore()

    def greet(k, carry):
        for peer in ((lax.rem(dp + k, PEERS), fsdp), (dp, lax.rem(fsdp + k, PEERS))):
            pl.semaphore_signal(barrier, inc=1, device_id=peer, device_id_type=MESH)
        return carry

    lax.fori_loop(1, PEERS, greet, 0)

    ring_half, ring_part = z // 4, lax.rem(z, 4)
    ring_place = (1 - ring_half) * (y * 4 + x) + ring_half * (x * 4 + y)
    own_ring = pltpu.make_async_copy(
        weight.at[core, ring_half, ring_part, :, :, pl.ds(*RING)],
        ring.at[ring_half, core, ring_place, ring_part],
        local_sem.at[1],
    )
    own_ring.start()
    own = []
    for j, (start, width) in enumerate(CHUNKS):
        for half, (line, place) in enumerate(((y, x), (x, y))):
            copy = pltpu.make_async_copy(
                weight.at[core, half, :, :, :, pl.ds(start, width)],
                chunk(j).at[half, core, line, place],
                local_sem.at[2 + 2 * j + half],
            )
            copy.start()
            own.append(copy)

    loads = [
        pltpu.make_async_copy(source, landing, local_sem.at[2 + 2 * len(CHUNKS) + n])
        for n, (source, landing) in enumerate(
            ((target_in, target), (segment_in, segment), (gain_in, gain), (hidden, raw))
        )
    ]
    for copy in loads:
        copy.start()

    def send(view, device, send_sem, recv_sem):
        pltpu.make_async_remote_copy(
            src_ref=view, dst_ref=view, send_sem=send_sem, recv_sem=recv_sem,
            device_id=device, device_id_type=MESH,
        ).start()

    def landed(view, sem):
        pltpu.make_async_copy(view, view, sem).wait()

    low, high = pl.ds(0, 2), pl.ds(2, 2)

    def near(j):
        g, s, r = chunk(j), g_send.at[j], g_recv.at[j, NEAR]
        own[2 * j].wait()
        own[2 * j + 1].wait()
        send(g.at[0, core, y, x], to_x_up, s, r)
        send(g.at[0, core, y, x], to_x_down, s, r)
        send(g.at[1, core, x, y], to_y_up, s, r)
        send(g.at[1, core, x, y], to_y_down, s, r)
        if j in DIRECT:
            send(g.at[0, core, y, x], (dp, y * 4 + x_far), s, r)
            send(g.at[1, core, x, y], (dp, y_far * 4 + x), s, r)

    def far(j):
        g, s, r = chunk(j), g_send.at[j], g_recv.at[j, FAR]
        landed(g.at[0, core, y], g_recv.at[j, NEAR])
        send(g.at[0, core, y, x_down, low], to_x_up, s, r)
        send(g.at[0, core, y, x_up, high], to_x_down, s, r)
        send(g.at[1, core, x, y_down, low], to_y_up, s, r)
        send(g.at[1, core, x, y_up, high], to_y_down, s, r)

    def lines(j):
        g, s, r, t = chunk(j), g_send.at[j], g_recv.at[j, LINE], g_recv.at[j, TWIN]
        if j in DIRECT:
            landed(g.at[0, core, pl.ds(0, 2), pl.ds(0, 3)], g_recv.at[j, NEAR])
        else:
            landed(g.at[0, core, y, low], g_recv.at[j, FAR])
        send(g.at[0, core, y], to_y_up, s, r)
        send(g.at[0, core, y], to_y_down, s, r)
        send(g.at[1, core, x], to_x_up, s, r)
        send(g.at[1, core, x], to_x_down, s, r)
        send(g.at[0, core, y], sibling, s, t)
        send(g.at[1, core, x], sibling, s, t)

    def pass_lines(j):
        g, s, r, t = chunk(j), g_send.at[j], g_recv.at[j, LAST], g_recv.at[j, TWIN]
        landed(g.at[0, core], g_recv.at[j, LINE])
        send(g.at[0, core, y_down, low], to_y_up, s, r)
        send(g.at[0, core, y_up, high], to_y_down, s, r)
        send(g.at[1, core, x_down, low], to_x_up, s, r)
        send(g.at[1, core, x_up, high], to_x_down, s, r)
        send(g.at[0, core, y_down], sibling, s, t)
        send(g.at[0, core, y_up], sibling, s, t)
        send(g.at[1, core, x_down], sibling, s, t)
        send(g.at[1, core, x_up], sibling, s, t)

    def last_lines(j):
        g, s, t = chunk(j), g_send.at[j], g_recv.at[j, TWIN_LAST]
        landed(g.at[0, core, low], g_recv.at[j, LAST])
        send(g.at[0, core, y_far], sibling, s, t)
        send(g.at[1, core, x_far], sibling, s, t)

    def twin(j):
        landed(chunk(j).at[:, other, pl.ds(0, 3)], g_recv.at[j, TWIN])

    def twin_last(j):
        landed(chunk(j).at[:, other, 0], g_recv.at[j, TWIN_LAST])

    def ring_at(where, h):
        return ring.at[where // 4, core, :, lax.rem(where, 4), h]

    def z_up(n):
        return lax.rem(z + n, 8)

    def z_down(n):
        return lax.rem(z + 8 - n, 8)

    def plane(h):
        view = ring.at[ring_half, core, ring_place, ring_part, h]

        def ship(k, carry):
            send(view, (dp, lax.rem(fsdp + k, PEERS)), z_send.at[0], z_recv.at[1 + h])
            return carry

        lax.fori_loop(1, PEERS, ship, 0)

    def to_sibling(where, h):
        send(ring_at(where, h), sibling, z_send.at[1], z_recv.at[0])

    def ring_start(h):
        landed(ring.at[ring_half, core, pl.ds(0, 15), ring_part, h], z_recv.at[1 + h])
        send(ring_at(z, h), to_z_up, z_send.at[1], z_recv.at[3 + h])
        send(ring_at(z, h), to_z_down, z_send.at[1], z_recv.at[3 + h])
        to_sibling(z, h)

    def ring_step(n, h):
        landed(ring.at[ring_half, core, :, ring_part], z_recv.at[2 * n + 1 + h])
        sem = z_recv.at[2 * n + 3 + h] if n < 3 else z_recv.at[9]
        if n < 3 or h == 0:
            send(ring_at(z_down(n), h), to_z_up, z_send.at[1], sem)
        if n < 3 or h == 1:
            send(ring_at(z_up(n), h), to_z_down, z_send.at[1], sem)
        to_sibling(z_down(n), h)
        to_sibling(z_up(n), h)

    def ring_end():
        landed(ring.at[ring_half, core, :, ring_part], z_recv.at[9])
        to_sibling(z_up(4), 0)
        to_sibling(z_up(4), 1)

    def ring_twin():
        landed(ring.at[:, other], z_recv.at[0])

    def plan():
        loads[0].wait()
        loads[1].wait()
        goal = target[...]
        shard, slot = goal >> 12, goal & (ROWS - 1)
        chosen = lax.broadcasted_iota(jnp.int32, (PEERS, ROWS), 0) == shard
        onehot = chosen.astype(jnp.float32)
        earlier = (
            lax.broadcasted_iota(jnp.int32, (ROWS, ROWS), 0)
            < lax.broadcasted_iota(jnp.int32, (ROWS, ROWS), 1)
        ).astype(jnp.bfloat16)
        before = nn(onehot.astype(jnp.bfloat16), earlier)
        rank = jnp.sum(onehot * before, axis=0, keepdims=True).astype(jnp.int32)
        bucket = shard * CAPACITY + rank
        spread[...] = (
            lax.broadcasted_iota(jnp.int32, (PEERS * CAPACITY, ROWS), 0) == bucket
        ).astype(jnp.bfloat16)
        lane = rank + CAPACITY * lax.rem(dp, 4)
        place = (lax.broadcasted_iota(jnp.int32, (128, ROWS), 0) == lane).astype(jnp.bfloat16)
        marks = (onehot * (slot + 1).astype(jnp.float32)).astype(jnp.bfloat16)
        table = nt(marks, place)
        slots_out[...] = jnp.broadcast_to(table[:, None, :], (PEERS, 8, 128))
        ids = jnp.broadcast_to(segment[...].astype(jnp.float32), (ROWS, ROWS))
        causal = lax.broadcasted_iota(jnp.int32, (ROWS, ROWS), 1) <= lax.broadcasted_iota(
            jnp.int32, (ROWS, ROWS), 0
        )
        mask[...] = ((ids == ids.T) & causal).astype(jnp.float32)

    def to_peers(source, landing, send_sem, recv_sem):
        def ship(k, carry):
            peer = lax.rem(dp + k, PEERS)
            pltpu.make_async_remote_copy(
                src_ref=source.at[peer], dst_ref=landing.at[dp],
                send_sem=send_sem, recv_sem=recv_sem,
                device_id=(peer, fsdp), device_id_type=MESH,
            ).start()
            return carry

        lax.fori_loop(1, PEERS, ship, 0)
        landing[dp] = source[dp]

    def from_peers(landing, recv_sem):
        landed(landing.at[pl.ds(0, PEERS - 1)], recv_sem)

    def plan_arrivals():
        from_peers(slots_in, s_sem.at[1])
        wanted = lax.broadcasted_iota(jnp.int32, (ROWS, 128), 0) + 1
        for t in range(4):
            row = slots_in[4 * t] + slots_in[4 * t + 1] + slots_in[4 * t + 2] + slots_in[4 * t + 3]
            row = row[0:1].astype(jnp.int32)
            collect[:, t * 128 : (t + 1) * 128] = (wanted == row).astype(jnp.bfloat16)

    def normalise():
        loads[2].wait()
        loads[3].wait()

        def some(i, carry):
            rows = pl.ds(pl.multiple_of(i * 16, 16), 16)
            floats = raw[rows, :].astype(jnp.float32)
            scale = lax.rsqrt(jnp.mean(floats * floats, axis=1, keepdims=True) + EPS)
            for shard in range(16):
                for c in range(2):
                    for half in range(2):
                        a = shard * 512 + c * 256 + half * 128
                        at = (1 - half) * shard + half * (shard % 4 * 4 + shard // 4)
                        b = ((half * 2 + c) * 16 + at) * 128
                        part = raw[rows, a : a + 128].astype(jnp.float32)
                        normed[rows, b : b + 128] = (part * scale * gain[:, a : a + 128]).astype(
                            jnp.bfloat16
                        )
            return carry

        lax.fori_loop(0, ROWS // 16, some, 0)

    def project_ring():
        total[5] = jnp.zeros((ROWS, 256), jnp.float32)

        def some(i, carry):
            columns = pl.ds(pl.multiple_of(i * 2048, 2048), 2048)
            block = ring[i // 2, lax.rem(i, 2)].reshape(2048, 256)
            total[5] += nn(normed[:, columns], block)
            return carry

        lax.fori_loop(0, 4, some, 0)

    def project_lines(j, c, mine):
        g, width = chunk(j), CHUNKS[j][1]
        sums = None
        for half in range(2):
            for line in mine[half]:
                first = ((half * 2 + c) * 16 + line * 4) * 128
                columns = pl.ds(pl.multiple_of(first, 512), 512)
                part = nn(normed[:, columns], g[half, c, line].reshape(512, width))
                sums = part if sums is None else sums + part
        return sums

    near_lines, far_lines = ((y, y_up, y_down), (x, x_up, x_down)), ((y_far,), (x_far,))

    def project_own(j):
        total[j, :, : CHUNKS[j][1]] = project_lines(j, core, near_lines)

    def project_twin(j):
        twin(j)
        total[j, :, : CHUNKS[j][1]] += project_lines(j, other, near_lines)

    def project_last(j):
        sums = project_lines(j, core, far_lines)
        twin_last(j)
        total[j, :, : CHUNKS[j][1]] += sums + project_lines(j, other, far_lines)

    def keep():
        keys[...] = total[0, :, :HEAD].astype(jnp.bfloat16)
        values[...] = total[0, :, HEAD:].astype(jnp.bfloat16)

    def group(n):
        if n == 5:
            return out_wide.at[2], in_wide.at[2], 256, RING[0]
        if n < 3:
            return out_wide.at[n - 1], in_wide.at[n - 1], 256, CHUNKS[n][0]
        return out_narrow.at[n - 3], in_narrow.at[n - 3], 128, CHUNKS[n][0]

    def attend(n):
        outgoing, incoming, width, start = group(n)
        contexts = []
        for h in range(width // HEAD):
            query = total[n, :, h * HEAD : (h + 1) * HEAD].astype(jnp.bfloat16)
            scores = nt(query, keys[...]) * HEAD ** (-0.5)
            scores = jnp.where(mask[...] > 0.5, scores, -1e30)
            expos = jnp.exp(scores - jnp.max(scores, axis=1, keepdims=True))
            weights = (expos / jnp.sum(expos, axis=1, keepdims=True)).astype(jnp.bfloat16)
            contexts.append(nn(weights, values[...]).astype(jnp.bfloat16))
        context = jnp.concatenate(contexts, axis=1) if len(contexts) > 1 else contexts[0]
        outgoing[...] = nn(spread[...], context).astype(jnp.bfloat16).reshape(PEERS, CAPACITY, width)
        to_peers(outgoing, incoming, a_send.at[n - 1], a_recv.at[n - 1])

    def deliver(n):
        outgoing, incoming, width, start = group(n)
        from_peers(incoming, a_recv.at[n - 1])
        rows = incoming[...].reshape(PEERS * CAPACITY, width)
        out[:, start : start + width] = nn(collect[...], rows).astype(jnp.bfloat16)

    pl.semaphore_wait(barrier, 2 * (PEERS - 1))
    near(0)
    own_ring.wait()
    plane(0)
    plane(1)
    near(1)
    near(2)
    plan()
    to_peers(slots_out, slots_in, s_sem.at[0], s_sem.at[1])
    normalise()
    lines(0)
    ring_start(0)
    ring_start(1)
    lines(1)
    far(2)
    ring_step(1, 0)
    ring_step(1, 1)
    plan_arrivals()
    pass_lines(0)
    project_own(0)
    ring_step(2, 0)
    project_twin(0)
    pass_lines(1)
    lines(2)
    near(3)
    near(4)
    ring_step(2, 1)
    project_own(1)
    last_lines(0)
    project_last(0)
    keep()
    ring_step(3, 0)
    project_twin(1)
    ring_step(3, 1)
    last_lines(1)
    project_last(1)
    attend(1)
    ring_end()
    pass_lines(2)
    lines(3)
    lines(4)
    ring_twin()
    project_ring()
    attend(5)
    project_own(2)
    project_twin(2)
    last_lines(2)
    pass_lines(3)
    project_last(2)
    attend(2)
    project_own(3)
    pass_lines(4)
    project_twin(3)
    last_lines(3)
    project_last(3)
    attend(3)
    project_own(4)
    project_twin(4)
    last_lines(4)
    project_last(4)
    attend(4)
    deliver(1)
    deliver(5)
    deliver(2)
    deliver(3)
    deliver(4)
    for j, (start, width) in enumerate(CHUNKS):
        landed(raw.at[pl.ds(0, width), pl.ds(0, 7936)], g_send.at[j])
    landed(raw.at[pl.ds(0, 16), pl.ds(0, 7680)], z_send.at[0])
    landed(raw.at[pl.ds(0, 240)], z_send.at[1])
    landed(slots_out.at[pl.ds(0, PEERS - 1)], s_sem.at[0])
    for n in range(1, 6):
        landed(group(n)[0].at[pl.ds(0, PEERS - 1)], a_send.at[n - 1])


def per_device(hidden, gain, qkv_weight, owner_segment, target_row):
    any_space = pl.BlockSpec(memory_space=pl.ANY)
    vmem = pl.BlockSpec(memory_space=pltpu.VMEM)
    bf16, f32 = jnp.bfloat16, jnp.float32
    dma = pltpu.SemaphoreType.DMA
    return pl.pallas_call(
        kernel,
        out_shape=pltpu.VMEM((ROWS, COLUMNS), bf16),
        in_specs=[any_space] * 5,
        out_specs=vmem,
        scratch_shapes=[
            pltpu.VMEM((3, 2, 2, 4, 4, 4, 2, 16, 256), bf16),
            pltpu.VMEM((2, 2, 2, 4, 4, 4, 2, 16, 128), bf16),
            pltpu.VMEM((2, 2, 16, 4, 2, 16, 256), bf16),
            pltpu.VMEM((ROWS, FEATURES), bf16),
            pltpu.VMEM((ROWS, FEATURES), bf16),
            pltpu.VMEM((1, FEATURES), f32),
            pltpu.VMEM((1, ROWS), jnp.int32),
            pltpu.VMEM((1, ROWS), jnp.int32),
            pltpu.VMEM((6, ROWS, 256), f32),
            pltpu.VMEM((ROWS, HEAD), bf16),
            pltpu.VMEM((ROWS, HEAD), bf16),
            pltpu.VMEM((ROWS, ROWS), f32),
            pltpu.VMEM((PEERS * CAPACITY, ROWS), bf16),
            pltpu.VMEM((ROWS, PEERS * CAPACITY), bf16),
            pltpu.VMEM((3, PEERS, CAPACITY, 256), bf16),
            pltpu.VMEM((3, PEERS, CAPACITY, 256), bf16),
            pltpu.VMEM((2, PEERS, CAPACITY, 128), bf16),
            pltpu.VMEM((2, PEERS, CAPACITY, 128), bf16),
            pltpu.VMEM((PEERS, 8, 128), f32),
            pltpu.VMEM((PEERS, 8, 128), f32),
            dma((6 + 2 * len(CHUNKS),)),
            dma((len(CHUNKS),)),
            dma((len(CHUNKS), 6)),
            dma((2,)),
            dma((10,)),
            dma((5,)),
            dma((5,)),
            dma((2,)),
        ],
        compiler_params=pltpu.CompilerParams(
            collective_id=0, has_side_effects=True, vmem_limit_bytes=56 << 20
        ),
        cost_estimate=pl.CostEstimate(
            flops=2 * ROWS * FEATURES * 1280, bytes_accessed=6 << 20, transcendentals=8 * ROWS * ROWS
        ),
    )(
        hidden,
        gain.reshape(1, FEATURES),
        qkv_weight.reshape(2, 2, 4, 2, 16, 1280),
        owner_segment.reshape(1, ROWS),
        target_row.reshape(1, ROWS),
    )


def solution(mesh):
    in_specs = (P(("dp", "fsdp"), None), P(), P("fsdp", None), P(("dp", "fsdp")), P(("dp", "fsdp")))
    out_specs = P(("dp", "fsdp"), None)
    return jax.shard_map(
        per_device, mesh=mesh, in_specs=in_specs, out_specs=out_specs, check_vma=False
    )
```

```python
import jax
import jax.numpy as jnp
from jax import lax
from jax.experimental import pallas as pl
from jax.experimental.pallas import tpu as pltpu
from jax.sharding import PartitionSpec as P

MESH = pl.DeviceIdType.MESH
HEAD = 128
EPS = 1e-05
ROWS = 256
FEATURES = 8192
PEERS = 16
CAPACITY = 32
CHUNKS = ((1024, 256), (0, 256), (512, 256), (768, 128), (896, 128))
RING = (256, 256)
COLUMNS = 1024
DIRECT = (0, 1, 3, 4)
NEAR, FAR, LINE, LAST, TWIN, TWIN_LAST = range(6)


def nt(a, b):
    return lax.dot_general(a, b, (((1,), (1,)), ((), ())), preferred_element_type=jnp.float32)


def nn(a, b):
    return jnp.dot(a, b, preferred_element_type=jnp.float32)


def kernel(
    hidden, gain_in, weight, segment_in, target_in, out,
    wide, narrow, ring, raw, normed, gain, segment, target, total, keys, values, mask, spread, collect,
    out_wide, in_wide, out_narrow, in_narrow, slots_out, slots_in,
    local_sem, g_send, g_recv, z_send, z_recv, a_send, a_recv, s_sem, word,
):
    dp, fsdp = lax.axis_index("dp"), lax.axis_index("fsdp")
    z, core = dp // 2, lax.rem(dp, 2)
    y, x = fsdp // 4, lax.rem(fsdp, 4)
    other = 1 - core
    x_up, x_down, x_far = lax.rem(x + 1, 4), lax.rem(x + 3, 4), lax.rem(x + 2, 4)
    y_up, y_down, y_far = lax.rem(y + 1, 4), lax.rem(y + 3, 4), lax.rem(y + 2, 4)
    to_x_up, to_x_down = (dp, y * 4 + x_up), (dp, y * 4 + x_down)
    to_y_up, to_y_down = (dp, y_up * 4 + x), (dp, y_down * 4 + x)
    to_z_up = (lax.rem(z + 1, 8) * 2 + core, fsdp)
    to_z_down = (lax.rem(z + 7, 8) * 2 + core, fsdp)
    sibling = (dp + other - core, fsdp)
    to_x_far, to_y_far = (dp, y * 4 + x_far), (dp, y_far * 4 + x)

    def chunk(j):
        return wide.at[j] if j < 3 else narrow.at[j - 3]

    barrier = pltpu.get_barrier_semaphore()

    for peer in (
        to_x_up, to_x_down, to_y_up, to_y_down, to_x_far, to_y_far, to_z_up, to_z_down, sibling
    ):
        pl.semaphore_signal(barrier, inc=1, device_id=peer, device_id_type=MESH)

    def tell(n):
        for peer in (to_z_up, to_z_down):
            pl.semaphore_signal(word.at[n], inc=1, device_id=peer, device_id_type=MESH)

    def hear(n):
        pl.semaphore_wait(word.at[n], 2)

    ring_half, ring_part = z // 4, lax.rem(z, 4)
    u, v = (1 - ring_half) * y + ring_half * x, (1 - ring_half) * x + ring_half * y
    own_ring = pltpu.make_async_copy(
        weight.at[core, ring_half, ring_part, :, :, pl.ds(*RING)],
        ring.at[ring_half, core, u, v, ring_part],
        local_sem.at[1],
    )
    own_ring.start()
    own = []
    for j, (start, width) in enumerate(CHUNKS):
        for half, (line, place) in enumerate(((y, x), (x, y))):
            copy = pltpu.make_async_copy(
                weight.at[core, half, :, :, :, pl.ds(start, width)],
                chunk(j).at[half, core, line, place],
                local_sem.at[2 + 2 * j + half],
            )
            copy.start()
            own.append(copy)

    loads = [
        pltpu.make_async_copy(source, landing, local_sem.at[2 + 2 * len(CHUNKS) + n])
        for n, (source, landing) in enumerate(
            ((target_in, target), (segment_in, segment), (gain_in, gain), (hidden, raw))
        )
    ]
    for copy in loads:
        copy.start()

    def send(view, device, send_sem, recv_sem):
        pltpu.make_async_remote_copy(
            src_ref=view, dst_ref=view, send_sem=send_sem, recv_sem=recv_sem,
            device_id=device, device_id_type=MESH,
        ).start()

    def landed(view, sem):
        pltpu.make_async_copy(view, view, sem).wait()

    low, high = pl.ds(0, 2), pl.ds(2, 2)

    def near(j):
        g, s, r = chunk(j), g_send.at[j], g_recv.at[j, NEAR]
        own[2 * j].wait()
        own[2 * j + 1].wait()
        send(g.at[0, core, y, x], to_x_up, s, r)
        send(g.at[0, core, y, x], to_x_down, s, r)
        send(g.at[1, core, x, y], to_y_up, s, r)
        send(g.at[1, core, x, y], to_y_down, s, r)
        if j in DIRECT:
            send(g.at[0, core, y, x], (dp, y * 4 + x_far), s, r)
            send(g.at[1, core, x, y], (dp, y_far * 4 + x), s, r)

    def far(j):
        g, s, r = chunk(j), g_send.at[j], g_recv.at[j, FAR]
        landed(g.at[0, core, y], g_recv.at[j, NEAR])
        send(g.at[0, core, y, x_down, low], to_x_up, s, r)
        send(g.at[0, core, y, x_up, high], to_x_down, s, r)
        send(g.at[1, core, x, y_down, low], to_y_up, s, r)
        send(g.at[1, core, x, y_up, high], to_y_down, s, r)

    def lines(j):
        g, s, r, t = chunk(j), g_send.at[j], g_recv.at[j, LINE], g_recv.at[j, TWIN]
        if j in DIRECT:
            landed(g.at[0, core, pl.ds(0, 2), pl.ds(0, 3)], g_recv.at[j, NEAR])
        else:
            landed(g.at[0, core, y, low], g_recv.at[j, FAR])
        send(g.at[0, core, y], to_y_up, s, r)
        send(g.at[0, core, y], to_y_down, s, r)
        send(g.at[1, core, x], to_x_up, s, r)
        send(g.at[1, core, x], to_x_down, s, r)
        send(g.at[0, core, y], sibling, s, t)
        send(g.at[1, core, x], sibling, s, t)

    def pass_lines(j):
        g, s, r, t = chunk(j), g_send.at[j], g_recv.at[j, LAST], g_recv.at[j, TWIN]
        landed(g.at[0, core], g_recv.at[j, LINE])
        send(g.at[0, core, y_down, low], to_y_up, s, r)
        send(g.at[0, core, y_up, high], to_y_down, s, r)
        send(g.at[1, core, x_down, low], to_x_up, s, r)
        send(g.at[1, core, x_up, high], to_x_down, s, r)
        send(g.at[0, core, y_down], sibling, s, t)
        send(g.at[0, core, y_up], sibling, s, t)
        send(g.at[1, core, x_down], sibling, s, t)
        send(g.at[1, core, x_up], sibling, s, t)

    def last_lines(j):
        g, s, t = chunk(j), g_send.at[j], g_recv.at[j, TWIN_LAST]
        landed(g.at[0, core, low], g_recv.at[j, LAST])
        send(g.at[0, core, y_far], sibling, s, t)
        send(g.at[1, core, x_far], sibling, s, t)

    def twin(j):
        landed(chunk(j).at[:, other, pl.ds(0, 3)], g_recv.at[j, TWIN])

    def twin_last(j):
        landed(chunk(j).at[:, other, 0], g_recv.at[j, TWIN_LAST])

    def ring_at(where, h):
        return ring.at[where // 4, core, :, :, lax.rem(where, 4), h]

    def z_up(n):
        return lax.rem(z + n, 8)

    def z_down(n):
        return lax.rem(z + 8 - n, 8)

    def beside(k, along):
        u_to, v_to = lax.rem(u + k * (1 - along), 4), lax.rem(v + k * along, 4)
        return (dp, (1 - ring_half) * (u_to * 4 + v_to) + ring_half * (v_to * 4 + u_to))

    def plane(h):
        for k in (1, 3, 2):
            view = ring.at[ring_half, core, u, v, ring_part, h]
            send(view, beside(k, 1 - h), z_send.at[0], z_recv.at[10 + h])

    def plane_lines(h):
        view = ring.at[ring_half, core, u, pl.ds(0, 3), ring_part, h]
        landed(view, z_recv.at[10 + h])
        if h == 0:
            view = ring.at[ring_half, core, u, :, ring_part, h]
        else:
            view = ring.at[ring_half, core, :, v, ring_part, h]
        for k in (1, 3, 2):
            send(view, beside(k, h), z_send.at[0], z_recv.at[1 + h])

    def to_sibling(where, h):
        send(ring_at(where, h), sibling, z_send.at[1], z_recv.at[0])

    def ring_start(h):
        landed(ring.at[ring_half, core, pl.ds(0, 3), :, ring_part, h], z_recv.at[1 + h])
        send(ring_at(z, h), to_z_up, z_send.at[1], z_recv.at[3 + h])
        send(ring_at(z, h), to_z_down, z_send.at[1], z_recv.at[3 + h])
        to_sibling(z, h)

    def ring_step(n, h):
        landed(ring.at[ring_half, core, :, :, ring_part], z_recv.at[2 * n + 1 + h])
        sem = z_recv.at[2 * n + 3 + h] if n < 3 else z_recv.at[9]
        if n < 3 or h == 0:
            send(ring_at(z_down(n), h), to_z_up, z_send.at[1], sem)
        if n < 3 or h == 1:
            send(ring_at(z_up(n), h), to_z_down, z_send.at[1], sem)
        to_sibling(z_down(n), h)
        to_sibling(z_up(n), h)

    def ring_end():
        landed(ring.at[ring_half, core, :, :, ring_part], z_recv.at[9])
        to_sibling(z_up(4), 0)
        to_sibling(z_up(4), 1)

    def ring_twin():
        landed(ring.at[:, other], z_recv.at[0])

    def plan():
        loads[0].wait()
        loads[1].wait()
        goal = target[...]
        shard, slot = goal >> 12, goal & (ROWS - 1)
        chosen = lax.broadcasted_iota(jnp.int32, (PEERS, ROWS), 0) == shard
        onehot = chosen.astype(jnp.float32)
        earlier = (
            lax.broadcasted_iota(jnp.int32, (ROWS, ROWS), 0)
            < lax.broadcasted_iota(jnp.int32, (ROWS, ROWS), 1)
        ).astype(jnp.bfloat16)
        before = nn(onehot.astype(jnp.bfloat16), earlier)
        rank = jnp.sum(onehot * before, axis=0, keepdims=True).astype(jnp.int32)
        bucket = shard * CAPACITY + rank
        spread[...] = (
            lax.broadcasted_iota(jnp.int32, (PEERS * CAPACITY, ROWS), 0) == bucket
        ).astype(jnp.bfloat16)
        lane = rank + CAPACITY * lax.rem(dp, 4)
        place = (lax.broadcasted_iota(jnp.int32, (128, ROWS), 0) == lane).astype(jnp.bfloat16)
        marks = (onehot * (slot + 1).astype(jnp.float32)).astype(jnp.bfloat16)
        table = nt(marks, place)
        slots_out[...] = jnp.broadcast_to(table[:, None, :], (PEERS, 8, 128))
        ids = jnp.broadcast_to(segment[...].astype(jnp.float32), (ROWS, ROWS))
        causal = lax.broadcasted_iota(jnp.int32, (ROWS, ROWS), 1) <= lax.broadcasted_iota(
            jnp.int32, (ROWS, ROWS), 0
        )
        mask[...] = ((ids == ids.T) & causal).astype(jnp.float32)

    def to_peers(source, landing, send_sem, recv_sem):
        def ship(k, carry):
            peer = lax.rem(dp + k, PEERS)
            pltpu.make_async_remote_copy(
                src_ref=source.at[peer], dst_ref=landing.at[dp],
                send_sem=send_sem, recv_sem=recv_sem,
                device_id=(peer, fsdp), device_id_type=MESH,
            ).start()
            return carry

        lax.fori_loop(1, PEERS, ship, 0)
        landing[dp] = source[dp]

    def from_peers(landing, recv_sem):
        landed(landing.at[pl.ds(0, PEERS - 1)], recv_sem)

    def plan_arrivals():
        from_peers(slots_in, s_sem.at[1])
        wanted = lax.broadcasted_iota(jnp.int32, (ROWS, 128), 0) + 1
        for t in range(4):
            row = slots_in[4 * t] + slots_in[4 * t + 1] + slots_in[4 * t + 2] + slots_in[4 * t + 3]
            row = row[0:1].astype(jnp.int32)
            collect[:, t * 128 : (t + 1) * 128] = (wanted == row).astype(jnp.bfloat16)

    def normalise(part):
        if part == 0:
            loads[2].wait()
            loads[3].wait()

        def some(i, carry):
            rows = pl.ds(pl.multiple_of(i * 16, 16), 16)
            floats = raw[rows, :].astype(jnp.float32)
            scale = lax.rsqrt(jnp.mean(floats * floats, axis=1, keepdims=True) + EPS)
            for shard in range(16):
                for c in range(2):
                    for half in range(2):
                        a = shard * 512 + c * 256 + half * 128
                        at = (1 - half) * shard + half * (shard % 4 * 4 + shard // 4)
                        b = ((half * 2 + c) * 16 + at) * 128
                        part = raw[rows, a : a + 128].astype(jnp.float32)
                        normed[rows, b : b + 128] = (part * scale * gain[:, a : a + 128]).astype(
                            jnp.bfloat16
                        )
            return carry

        lax.fori_loop(part * 8, part * 8 + 8, some, 0)

    def project_ring():
        total[5] = jnp.zeros((ROWS, 256), jnp.float32)

        def some(i, carry):
            columns = pl.ds(pl.multiple_of(i * 2048, 2048), 2048)
            block = ring[i // 2, lax.rem(i, 2)].reshape(2048, 256)
            total[5] += nn(normed[:, columns], block)
            return carry

        lax.fori_loop(0, 4, some, 0)

    def project_lines(j, c, mine):
        g, width = chunk(j), CHUNKS[j][1]
        sums = None
        for half in range(2):
            for line in mine[half]:
                first = ((half * 2 + c) * 16 + line * 4) * 128
                columns = pl.ds(pl.multiple_of(first, 512), 512)
                part = nn(normed[:, columns], g[half, c, line].reshape(512, width))
                sums = part if sums is None else sums + part
        return sums

    near_lines, far_lines = ((y, y_up, y_down), (x, x_up, x_down)), ((y_far,), (x_far,))

    def project_own(j):
        total[j, :, : CHUNKS[j][1]] = project_lines(j, core, near_lines)

    def project_twin(j):
        twin(j)
        total[j, :, : CHUNKS[j][1]] += project_lines(j, other, near_lines)

    def project_last(j):
        sums = project_lines(j, core, far_lines)
        twin_last(j)
        total[j, :, : CHUNKS[j][1]] += sums + project_lines(j, other, far_lines)

    def keep():
        keys[...] = total[0, :, :HEAD].astype(jnp.bfloat16)
        values[...] = total[0, :, HEAD:].astype(jnp.bfloat16)

    def group(n):
        if n == 5:
            return out_wide.at[2], in_wide.at[2], 256, RING[0]
        if n < 3:
            return out_wide.at[n - 1], in_wide.at[n - 1], 256, CHUNKS[n][0]
        return out_narrow.at[n - 3], in_narrow.at[n - 3], 128, CHUNKS[n][0]

    def attend(n):
        outgoing, incoming, width, start = group(n)
        contexts = []
        for h in range(width // HEAD):
            query = total[n, :, h * HEAD : (h + 1) * HEAD].astype(jnp.bfloat16)
            scores = nt(query, keys[...]) * HEAD ** (-0.5)
            scores = jnp.where(mask[...] > 0.5, scores, -1e30)
            expos = jnp.exp(scores - jnp.max(scores, axis=1, keepdims=True))
            weights = (expos / jnp.sum(expos, axis=1, keepdims=True)).astype(jnp.bfloat16)
            contexts.append(nn(weights, values[...]).astype(jnp.bfloat16))
        context = jnp.concatenate(contexts, axis=1) if len(contexts) > 1 else contexts[0]
        outgoing[...] = nn(spread[...], context).astype(jnp.bfloat16).reshape(PEERS, CAPACITY, width)
        to_peers(outgoing, incoming, a_send.at[n - 1], a_recv.at[n - 1])

    def deliver(n):
        outgoing, incoming, width, start = group(n)
        from_peers(incoming, a_recv.at[n - 1])
        rows = incoming[...].reshape(PEERS * CAPACITY, width)
        out[:, start : start + width] = nn(collect[...], rows).astype(jnp.bfloat16)

    pl.semaphore_wait(barrier, 9)
    tell(0)
    own_ring.wait()
    plane(0)
    plane(1)
    near(0)
    near(1)
    plan()
    normalise(0)
    plane_lines(0)
    plane_lines(1)
    near(2)
    normalise(1)
    lines(0)
    hear(0)
    tell(1)
    lines(1)
    ring_start(0)
    ring_start(1)
    far(2)
    hear(1)
    tell(2)
    ring_step(1, 0)
    pass_lines(0)
    ring_step(1, 1)
    project_own(0)
    hear(2)
    tell(3)
    project_twin(0)
    ring_step(2, 0)
    pass_lines(1)
    lines(2)
    near(3)
    near(4)
    ring_step(2, 1)
    project_own(1)
    hear(3)
    to_peers(slots_out, slots_in, s_sem.at[0], s_sem.at[1])
    last_lines(0)
    project_last(0)
    keep()
    ring_step(3, 0)
    project_twin(1)
    ring_step(3, 1)
    last_lines(1)
    project_last(1)
    attend(1)
    ring_end()
    plan_arrivals()
    pass_lines(2)
    lines(3)
    lines(4)
    ring_twin()
    project_ring()
    attend(5)
    project_own(2)
    project_twin(2)
    last_lines(2)
    pass_lines(3)
    project_last(2)
    attend(2)
    project_own(3)
    pass_lines(4)
    project_twin(3)
    last_lines(3)
    project_last(3)
    attend(3)
    project_own(4)
    project_twin(4)
    last_lines(4)
    project_last(4)
    attend(4)
    deliver(1)
    deliver(5)
    deliver(2)
    deliver(3)
    deliver(4)
    for j, (start, width) in enumerate(CHUNKS):
        landed(raw.at[pl.ds(0, width), pl.ds(0, 7936)], g_send.at[j])
    landed(raw.at[pl.ds(0, 16), pl.ds(0, 7680)], z_send.at[0])
    landed(raw.at[pl.ds(0, 240)], z_send.at[1])
    landed(slots_out.at[pl.ds(0, PEERS - 1)], s_sem.at[0])
    for n in range(1, 6):
        landed(group(n)[0].at[pl.ds(0, PEERS - 1)], a_send.at[n - 1])


def per_device(hidden, gain, qkv_weight, owner_segment, target_row):
    any_space = pl.BlockSpec(memory_space=pl.ANY)
    vmem = pl.BlockSpec(memory_space=pltpu.VMEM)
    bf16, f32 = jnp.bfloat16, jnp.float32
    dma = pltpu.SemaphoreType.DMA
    return pl.pallas_call(
        kernel,
        out_shape=pltpu.VMEM((ROWS, COLUMNS), bf16),
        in_specs=[any_space] * 5,
        out_specs=vmem,
        scratch_shapes=[
            pltpu.VMEM((3, 2, 2, 4, 4, 4, 2, 16, 256), bf16),
            pltpu.VMEM((2, 2, 2, 4, 4, 4, 2, 16, 128), bf16),
            pltpu.VMEM((2, 2, 4, 4, 4, 2, 16, 256), bf16),
            pltpu.VMEM((ROWS, FEATURES), bf16),
            pltpu.VMEM((ROWS, FEATURES), bf16),
            pltpu.VMEM((1, FEATURES), f32),
            pltpu.VMEM((1, ROWS), jnp.int32),
            pltpu.VMEM((1, ROWS), jnp.int32),
            pltpu.VMEM((6, ROWS, 256), f32),
            pltpu.VMEM((ROWS, HEAD), bf16),
            pltpu.VMEM((ROWS, HEAD), bf16),
            pltpu.VMEM((ROWS, ROWS), f32),
            pltpu.VMEM((PEERS * CAPACITY, ROWS), bf16),
            pltpu.VMEM((ROWS, PEERS * CAPACITY), bf16),
            pltpu.VMEM((3, PEERS, CAPACITY, 256), bf16),
            pltpu.VMEM((3, PEERS, CAPACITY, 256), bf16),
            pltpu.VMEM((2, PEERS, CAPACITY, 128), bf16),
            pltpu.VMEM((2, PEERS, CAPACITY, 128), bf16),
            pltpu.VMEM((PEERS, 8, 128), f32),
            pltpu.VMEM((PEERS, 8, 128), f32),
            dma((6 + 2 * len(CHUNKS),)),
            dma((len(CHUNKS),)),
            dma((len(CHUNKS), 6)),
            dma((2,)),
            dma((12,)),
            dma((5,)),
            dma((5,)),
            dma((2,)),
            pltpu.SemaphoreType.REGULAR((4,)),
        ],
        compiler_params=pltpu.CompilerParams(
            collective_id=0, has_side_effects=True, vmem_limit_bytes=56 << 20
        ),
        cost_estimate=pl.CostEstimate(
            flops=2 * ROWS * FEATURES * 1280, bytes_accessed=6 << 20, transcendentals=8 * ROWS * ROWS
        ),
    )(
        hidden,
        gain.reshape(1, FEATURES),
        qkv_weight.reshape(2, 2, 4, 2, 16, 1280),
        owner_segment.reshape(1, ROWS),
        target_row.reshape(1, ROWS),
    )


def solution(mesh):
    in_specs = (P(("dp", "fsdp"), None), P(), P("fsdp", None), P(("dp", "fsdp")), P(("dp", "fsdp")))
    out_specs = P(("dp", "fsdp"), None)
    return jax.shard_map(
        per_device, mesh=mesh, in_specs=in_specs, out_specs=out_specs, check_vma=False
    )
```

```python
import math

import jax
import jax.numpy as jnp
from jax import lax
from jax.experimental import pallas as pl
from jax.experimental.pallas import tpu as pltpu
from jax.sharding import PartitionSpec as P

MESH = pl.DeviceIdType.MESH
HEAD = 128
EPS = 1e-05
SCALE = HEAD ** (-0.5) * math.log2(math.e)
ROWS = 256
FEATURES = 8192
PEERS = 16
CAPACITY = 32
CHUNKS = ((1024, 256), (0, 256), (512, 256), (768, 128), (896, 128))
RING = (256, 256)
COLUMNS = 1024
DIRECT = (0, 1, 3, 4)
NEAR, FAR, LINE, LAST, TWIN, TWIN_LAST = range(6)


def nt(a, b):
    return lax.dot_general(a, b, (((1,), (1,)), ((), ())), preferred_element_type=jnp.float32)


def nn(a, b):
    return jnp.dot(a, b, preferred_element_type=jnp.float32)


def kernel(
    hidden, gain_in, weight, segment_in, target_in, out,
    wide, narrow, ring, raw, normed, gain, segment, target, total, keys, values, mask, spread, collect,
    out_wide, in_wide, out_narrow, in_narrow, slots_out, slots_in,
    local_sem, g_send, g_recv, z_send, z_recv, a_send, a_recv, s_sem, word,
):
    dp, fsdp = lax.axis_index("dp"), lax.axis_index("fsdp")
    z, core = dp // 2, lax.rem(dp, 2)
    y, x = fsdp // 4, lax.rem(fsdp, 4)
    other = 1 - core
    x_up, x_down, x_far = lax.rem(x + 1, 4), lax.rem(x + 3, 4), lax.rem(x + 2, 4)
    y_up, y_down, y_far = lax.rem(y + 1, 4), lax.rem(y + 3, 4), lax.rem(y + 2, 4)
    to_x_up, to_x_down = (dp, y * 4 + x_up), (dp, y * 4 + x_down)
    to_y_up, to_y_down = (dp, y_up * 4 + x), (dp, y_down * 4 + x)
    to_z_up = (lax.rem(z + 1, 8) * 2 + core, fsdp)
    to_z_down = (lax.rem(z + 7, 8) * 2 + core, fsdp)
    sibling = (dp + other - core, fsdp)
    to_x_far, to_y_far = (dp, y * 4 + x_far), (dp, y_far * 4 + x)

    def chunk(j):
        return wide.at[j] if j < 3 else narrow.at[j - 3]

    barrier = pltpu.get_barrier_semaphore()

    for peer in (
        to_x_up, to_x_down, to_y_up, to_y_down, to_x_far, to_y_far, to_z_up, to_z_down, sibling
    ):
        pl.semaphore_signal(barrier, inc=1, device_id=peer, device_id_type=MESH)

    def tell(n):
        for peer in (to_z_up, to_z_down):
            pl.semaphore_signal(word.at[n], inc=1, device_id=peer, device_id_type=MESH)

    def hear(n):
        pl.semaphore_wait(word.at[n], 2)

    ring_half, ring_part = z // 4, lax.rem(z, 4)
    u, v = (1 - ring_half) * y + ring_half * x, (1 - ring_half) * x + ring_half * y
    own_ring = pltpu.make_async_copy(
        weight.at[core, ring_half, ring_part, :, :, pl.ds(*RING)],
        ring.at[ring_half, core, u, v, ring_part],
        local_sem.at[2],
    )
    own_ring.start()
    for j, (start, width) in enumerate(CHUNKS):
        for half, (line, place) in enumerate(((y, x), (x, y))):
            pltpu.make_async_copy(
                weight.at[core, half, :, :, :, pl.ds(start, width)],
                chunk(j).at[half, core, line, place],
                local_sem.at[3],
            ).start()

    loads = [
        pltpu.make_async_copy(source, landing, sem)
        for source, landing, sem in (
            (target_in, target, local_sem.at[0]),
            (segment_in, segment, local_sem.at[1]),
            (gain_in, gain, local_sem.at[4]),
            (hidden, raw, local_sem.at[5]),
        )
    ]
    for copy in loads:
        copy.start()

    def send(view, device, send_sem, recv_sem):
        pltpu.make_async_remote_copy(
            src_ref=view, dst_ref=view, send_sem=send_sem, recv_sem=recv_sem,
            device_id=device, device_id_type=MESH,
        ).start()

    def landed(view, sem):
        pltpu.make_async_copy(view, view, sem).wait()

    low, high = pl.ds(0, 2), pl.ds(2, 2)

    def own_blocks():
        own_ring.wait()
        landed(raw.at[pl.ds(0, 32), pl.ds(0, FEATURES)], local_sem.at[3])

    def near(j):
        g, s, r = chunk(j), g_send.at[j], g_recv.at[j, NEAR]
        send(g.at[0, core, y, x], to_x_up, s, r)
        send(g.at[0, core, y, x], to_x_down, s, r)
        send(g.at[1, core, x, y], to_y_up, s, r)
        send(g.at[1, core, x, y], to_y_down, s, r)
        if j in DIRECT:
            send(g.at[0, core, y, x], (dp, y * 4 + x_far), s, r)
            send(g.at[1, core, x, y], (dp, y_far * 4 + x), s, r)

    def far(j):
        g, s, r = chunk(j), g_send.at[j], g_recv.at[j, FAR]
        landed(g.at[0, core, y], g_recv.at[j, NEAR])
        send(g.at[0, core, y, x_down, low], to_x_up, s, r)
        send(g.at[0, core, y, x_up, high], to_x_down, s, r)
        send(g.at[1, core, x, y_down, low], to_y_up, s, r)
        send(g.at[1, core, x, y_up, high], to_y_down, s, r)

    def lines(j):
        g, s, r, t = chunk(j), g_send.at[j], g_recv.at[j, LINE], g_recv.at[j, TWIN]
        if j in DIRECT:
            landed(g.at[0, core, pl.ds(0, 2), pl.ds(0, 3)], g_recv.at[j, NEAR])
        else:
            landed(g.at[0, core, y, low], g_recv.at[j, FAR])
        send(g.at[0, core, y], to_y_up, s, r)
        send(g.at[0, core, y], to_y_down, s, r)
        send(g.at[1, core, x], to_x_up, s, r)
        send(g.at[1, core, x], to_x_down, s, r)
        send(g.at[0, core, y], sibling, s, t)
        send(g.at[1, core, x], sibling, s, t)

    def pass_lines(j):
        g, s, r, t = chunk(j), g_send.at[j], g_recv.at[j, LAST], g_recv.at[j, TWIN]
        landed(g.at[0, core], g_recv.at[j, LINE])
        send(g.at[0, core, y_down, low], to_y_up, s, r)
        send(g.at[0, core, y_up, high], to_y_down, s, r)
        send(g.at[1, core, x_down, low], to_x_up, s, r)
        send(g.at[1, core, x_up, high], to_x_down, s, r)
        send(g.at[0, core, y_down], sibling, s, t)
        send(g.at[0, core, y_up], sibling, s, t)
        send(g.at[1, core, x_down], sibling, s, t)
        send(g.at[1, core, x_up], sibling, s, t)

    def last_lines(j):
        g, s, t = chunk(j), g_send.at[j], g_recv.at[j, TWIN_LAST]
        landed(g.at[0, core, low], g_recv.at[j, LAST])
        send(g.at[0, core, y_far], sibling, s, t)
        send(g.at[1, core, x_far], sibling, s, t)

    def twin(j):
        landed(chunk(j).at[:, other, pl.ds(0, 3)], g_recv.at[j, TWIN])

    def twin_last(j):
        landed(chunk(j).at[:, other, 0], g_recv.at[j, TWIN_LAST])

    def ring_at(where, h):
        return ring.at[where // 4, core, :, :, lax.rem(where, 4), h]

    def z_up(n):
        return lax.rem(z + n, 8)

    def z_down(n):
        return lax.rem(z + 8 - n, 8)

    def beside(k, along):
        u_to, v_to = lax.rem(u + k * (1 - along), 4), lax.rem(v + k * along, 4)
        return (dp, (1 - ring_half) * (u_to * 4 + v_to) + ring_half * (v_to * 4 + u_to))

    def plane(h):
        for k in (1, 3, 2):
            view = ring.at[ring_half, core, u, v, ring_part, h]
            send(view, beside(k, 1 - h), z_send.at[0], z_recv.at[10 + h])

    def plane_lines(h):
        view = ring.at[ring_half, core, u, pl.ds(0, 3), ring_part, h]
        landed(view, z_recv.at[10 + h])
        if h == 0:
            view = ring.at[ring_half, core, u, :, ring_part, h]
        else:
            view = ring.at[ring_half, core, :, v, ring_part, h]
        for k in (1, 3, 2):
            send(view, beside(k, h), z_send.at[0], z_recv.at[1 + h])

    def to_sibling(where, h):
        send(ring_at(where, h), sibling, z_send.at[1], z_recv.at[0])

    def ring_start(h):
        landed(ring.at[ring_half, core, pl.ds(0, 3), :, ring_part, h], z_recv.at[1 + h])
        send(ring_at(z, h), to_z_up, z_send.at[1], z_recv.at[3 + h])
        send(ring_at(z, h), to_z_down, z_send.at[1], z_recv.at[3 + h])
        to_sibling(z, h)

    def ring_step(n, h):
        landed(ring.at[ring_half, core, :, :, ring_part], z_recv.at[2 * n + 1 + h])
        sem = z_recv.at[2 * n + 3 + h] if n < 3 else z_recv.at[9]
        if n < 3 or h == 0:
            send(ring_at(z_down(n), h), to_z_up, z_send.at[1], sem)
        if n < 3 or h == 1:
            send(ring_at(z_up(n), h), to_z_down, z_send.at[1], sem)
        to_sibling(z_down(n), h)
        to_sibling(z_up(n), h)

    def ring_end():
        landed(ring.at[ring_half, core, :, :, ring_part], z_recv.at[9])
        to_sibling(z_up(4), 0)
        to_sibling(z_up(4), 1)

    def ring_twin():
        landed(ring.at[:, other], z_recv.at[0])

    def plan():
        loads[0].wait()
        loads[1].wait()
        goal = target[...]
        shard, slot = goal >> 12, goal & (ROWS - 1)
        chosen = lax.broadcasted_iota(jnp.int32, (PEERS, ROWS), 0) == shard
        onehot = chosen.astype(jnp.float32)
        earlier = (
            lax.broadcasted_iota(jnp.int32, (ROWS, ROWS), 0)
            < lax.broadcasted_iota(jnp.int32, (ROWS, ROWS), 1)
        ).astype(jnp.bfloat16)
        before = nn(onehot.astype(jnp.bfloat16), earlier)
        rank = jnp.sum(onehot * before, axis=0, keepdims=True).astype(jnp.int32)
        bucket = shard * CAPACITY + rank
        spread[...] = (
            lax.broadcasted_iota(jnp.int32, (PEERS * CAPACITY, ROWS), 0) == bucket
        ).astype(jnp.bfloat16)
        lane = rank + CAPACITY * lax.rem(dp, 4)
        place = (lax.broadcasted_iota(jnp.int32, (128, ROWS), 0) == lane).astype(jnp.bfloat16)
        marks = (onehot * (slot + 1).astype(jnp.float32)).astype(jnp.bfloat16)
        table = nt(marks, place)
        slots_out[...] = jnp.broadcast_to(table[:, None, :], (PEERS, 8, 128))
        ids = jnp.broadcast_to(segment[...].astype(jnp.float32), (ROWS, ROWS))
        causal = lax.broadcasted_iota(jnp.int32, (ROWS, ROWS), 1) <= lax.broadcasted_iota(
            jnp.int32, (ROWS, ROWS), 0
        )
        mask[...] = jnp.where((ids == ids.T) & causal, 0.0, -1e30)

    def to_peers(source, landing, send_sem, recv_sem):
        def ship(k, carry):
            peer = lax.rem(dp + 8 + (k + 1) // 2 * (1 - 2 * lax.rem(k, 2)), PEERS)
            pltpu.make_async_remote_copy(
                src_ref=source.at[peer], dst_ref=landing.at[dp],
                send_sem=send_sem, recv_sem=recv_sem,
                device_id=(peer, fsdp), device_id_type=MESH,
            ).start()
            return carry

        lax.fori_loop(0, PEERS - 1, ship, 0)
        landing[dp] = source[dp]

    def from_peers(landing, recv_sem):
        landed(landing.at[pl.ds(0, PEERS - 1)], recv_sem)

    def plan_arrivals():
        from_peers(slots_in, s_sem.at[1])
        wanted = lax.broadcasted_iota(jnp.int32, (ROWS, 128), 0) + 1
        for t in range(4):
            row = slots_in[4 * t] + slots_in[4 * t + 1] + slots_in[4 * t + 2] + slots_in[4 * t + 3]
            row = row[0:1].astype(jnp.int32)
            collect[:, t * 128 : (t + 1) * 128] = (wanted == row).astype(jnp.bfloat16)

    def normalise(part):
        if part == 0:
            loads[2].wait()
            loads[3].wait()

        def some(i, carry):
            rows = pl.ds(pl.multiple_of(i * 16, 16), 16)
            floats = raw[rows, :].astype(jnp.float32)
            scale = lax.rsqrt(jnp.mean(floats * floats, axis=1, keepdims=True) + EPS)
            for shard in range(16):
                for c in range(2):
                    for half in range(2):
                        a = shard * 512 + c * 256 + half * 128
                        at = (1 - half) * shard + half * (shard % 4 * 4 + shard // 4)
                        b = ((half * 2 + c) * 16 + at) * 128
                        part = raw[rows, a : a + 128].astype(jnp.float32)
                        normed[rows, b : b + 128] = (part * scale * gain[:, a : a + 128]).astype(
                            jnp.bfloat16
                        )
            return carry

        lax.fori_loop(part * 8, part * 8 + 8, some, 0)

    def project_ring():
        total[5] = jnp.zeros((ROWS, 256), jnp.float32)

        def some(i, carry):
            columns = pl.ds(pl.multiple_of(i * 2048, 2048), 2048)
            block = ring[i // 2, lax.rem(i, 2)].reshape(2048, 256)
            total[5] += nn(normed[:, columns], block)
            return carry

        lax.fori_loop(0, 4, some, 0)

    def project_lines(j, c, mine):
        g, width = chunk(j), CHUNKS[j][1]
        sums = None
        for half in range(2):
            for line in mine[half]:
                first = ((half * 2 + c) * 16 + line * 4) * 128
                columns = pl.ds(pl.multiple_of(first, 512), 512)
                part = nn(normed[:, columns], g[half, c, line].reshape(512, width))
                sums = part if sums is None else sums + part
        return sums

    near_lines, far_lines = ((y, y_up, y_down), (x, x_up, x_down)), ((y_far,), (x_far,))

    def project_own(j):
        total[j, :, : CHUNKS[j][1]] = project_lines(j, core, near_lines)

    def project_twin(j):
        twin(j)
        total[j, :, : CHUNKS[j][1]] += project_lines(j, other, near_lines)

    def project_last(j):
        sums = project_lines(j, core, far_lines)
        twin_last(j)
        total[j, :, : CHUNKS[j][1]] += sums + project_lines(j, other, far_lines)

    def keep():
        keys[...] = total[0, :, :HEAD].astype(jnp.bfloat16)
        values[...] = total[0, :, HEAD:].astype(jnp.bfloat16)

    def group(n):
        if n == 5:
            return out_wide.at[2], in_wide.at[2], 256, RING[0]
        if n < 3:
            return out_wide.at[n - 1], in_wide.at[n - 1], 256, CHUNKS[n][0]
        return out_narrow.at[n - 3], in_narrow.at[n - 3], 128, CHUNKS[n][0]

    def attend(n):
        outgoing, incoming, width, start = group(n)
        contexts = []
        for h in range(width // HEAD):
            query = total[n, :, h * HEAD : (h + 1) * HEAD].astype(jnp.bfloat16)
            scores = nt(query, keys[...]) + mask[...]
            expos = jnp.exp2((scores - jnp.max(scores, axis=1, keepdims=True)) * SCALE)
            weights = (expos * (1.0 / jnp.sum(expos, axis=1, keepdims=True))).astype(jnp.bfloat16)
            contexts.append(nn(weights, values[...]).astype(jnp.bfloat16))
        context = jnp.concatenate(contexts, axis=1) if len(contexts) > 1 else contexts[0]
        outgoing[...] = nn(spread[...], context).astype(jnp.bfloat16).reshape(PEERS, CAPACITY, width)
        to_peers(outgoing, incoming, a_send.at[0], a_recv.at[n - 1])

    def deliver(n):
        outgoing, incoming, width, start = group(n)
        from_peers(incoming, a_recv.at[n - 1])
        rows = incoming[...].reshape(PEERS * CAPACITY, width)
        out[:, start : start + width] = nn(collect[...], rows).astype(jnp.bfloat16)

    pl.semaphore_wait(barrier, 9)
    tell(0)
    own_blocks()
    plane(0)
    plane(1)
    near(0)
    near(1)
    plan()
    normalise(0)
    plane_lines(0)
    plane_lines(1)
    near(2)
    normalise(1)
    lines(0)
    hear(0)
    tell(1)
    lines(1)
    ring_start(0)
    ring_start(1)
    far(2)
    hear(1)
    tell(2)
    ring_step(1, 0)
    pass_lines(0)
    ring_step(1, 1)
    project_own(0)
    hear(2)
    tell(3)
    project_twin(0)
    ring_step(2, 0)
    pass_lines(1)
    lines(2)
    near(3)
    near(4)
    ring_step(2, 1)
    project_own(1)
    hear(3)
    to_peers(slots_out, slots_in, s_sem.at[0], s_sem.at[1])
    last_lines(0)
    project_last(0)
    keep()
    ring_step(3, 0)
    project_twin(1)
    ring_step(3, 1)
    last_lines(1)
    project_last(1)
    attend(1)
    ring_end()
    plan_arrivals()
    pass_lines(2)
    ring_twin()
    project_ring()
    lines(3)
    lines(4)
    attend(5)
    project_own(2)
    project_twin(2)
    last_lines(2)
    pass_lines(3)
    project_last(2)
    attend(2)
    project_own(3)
    pass_lines(4)
    project_twin(3)
    last_lines(3)
    project_last(3)
    attend(3)
    project_own(4)
    project_twin(4)
    last_lines(4)
    project_last(4)
    attend(4)
    deliver(1)
    deliver(5)
    deliver(2)
    deliver(3)
    deliver(4)
    for j, (start, width) in enumerate(CHUNKS):
        landed(raw.at[pl.ds(0, width), pl.ds(0, 7936)], g_send.at[j])
    landed(raw.at[pl.ds(0, 16), pl.ds(0, 7680)], z_send.at[0])
    landed(raw.at[pl.ds(0, 240)], z_send.at[1])
    landed(slots_out.at[pl.ds(0, PEERS - 1)], s_sem.at[0])
    landed(raw.at[pl.ds(0, 64), pl.ds(0, 7680)], a_send.at[0])

def per_device(hidden, gain, qkv_weight, owner_segment, target_row):
    any_space = pl.BlockSpec(memory_space=pl.ANY)
    vmem = pl.BlockSpec(memory_space=pltpu.VMEM)
    bf16, f32 = jnp.bfloat16, jnp.float32
    dma = pltpu.SemaphoreType.DMA
    return pl.pallas_call(
        kernel,
        out_shape=pltpu.VMEM((ROWS, COLUMNS), bf16),
        in_specs=[any_space] * 5,
        out_specs=vmem,
        scratch_shapes=[
            pltpu.VMEM((3, 2, 2, 4, 4, 4, 2, 16, 256), bf16),
            pltpu.VMEM((2, 2, 2, 4, 4, 4, 2, 16, 128), bf16),
            pltpu.VMEM((2, 2, 4, 4, 4, 2, 16, 256), bf16),
            pltpu.VMEM((ROWS, FEATURES), bf16),
            pltpu.VMEM((ROWS, FEATURES), bf16),
            pltpu.VMEM((1, FEATURES), f32),
            pltpu.VMEM((1, ROWS), jnp.int32),
            pltpu.VMEM((1, ROWS), jnp.int32),
            pltpu.VMEM((6, ROWS, 256), f32),
            pltpu.VMEM((ROWS, HEAD), bf16),
            pltpu.VMEM((ROWS, HEAD), bf16),
            pltpu.VMEM((ROWS, ROWS), f32),
            pltpu.VMEM((PEERS * CAPACITY, ROWS), bf16),
            pltpu.VMEM((ROWS, PEERS * CAPACITY), bf16),
            pltpu.VMEM((3, PEERS, CAPACITY, 256), bf16),
            pltpu.VMEM((3, PEERS, CAPACITY, 256), bf16),
            pltpu.VMEM((2, PEERS, CAPACITY, 128), bf16),
            pltpu.VMEM((2, PEERS, CAPACITY, 128), bf16),
            pltpu.VMEM((PEERS, 8, 128), f32),
            pltpu.VMEM((PEERS, 8, 128), f32),
            dma((6,)),
            dma((len(CHUNKS),)),
            dma((len(CHUNKS), 6)),
            dma((2,)),
            dma((12,)),
            dma((1,)),
            dma((5,)),
            dma((2,)),
            pltpu.SemaphoreType.REGULAR((4,)),
        ],
        compiler_params=pltpu.CompilerParams(
            collective_id=0, has_side_effects=True, vmem_limit_bytes=56 << 20
        ),
        cost_estimate=pl.CostEstimate(
            flops=2 * ROWS * FEATURES * 1280, bytes_accessed=6 << 20, transcendentals=8 * ROWS * ROWS
        ),
    )(
        hidden,
        gain.reshape(1, FEATURES),
        qkv_weight.reshape(2, 2, 4, 2, 16, 1280),
        owner_segment.reshape(1, ROWS),
        target_row.reshape(1, ROWS),
    )


def solution(mesh):
    in_specs = (P(("dp", "fsdp"), None), P(), P("fsdp", None), P(("dp", "fsdp")), P(("dp", "fsdp")))
    out_specs = P(("dp", "fsdp"), None)
    return jax.shard_map(
        per_device, mesh=mesh, in_specs=in_specs, out_specs=out_specs, check_vma=False
    )
```

```python
import jax
import jax.numpy as jnp
from jax import lax
from jax.experimental import pallas as pl
from jax.experimental.pallas import tpu as pltpu
from jax.sharding import PartitionSpec as P

MESH = pl.DeviceIdType.MESH
HEAD = 128
EPS = 1e-05
ROWS = 256
FEATURES = 8192
PEERS = 16
CAPACITY = 32
CHUNKS = ((1024, 256), (0, 256), (512, 256), (768, 128), (896, 128))
RING = (256, 256)
COLUMNS = 1024
DIRECT = (0, 1, 3, 4)
NEAR, FAR, LINE, LAST, TWIN, TWIN_LAST = range(6)


def nt(a, b):
    return lax.dot_general(a, b, (((1,), (1,)), ((), ())), preferred_element_type=jnp.float32)


def nn(a, b):
    return jnp.dot(a, b, preferred_element_type=jnp.float32)


def kernel(
    hidden, gain_in, weight, segment_in, target_in, out,
    wide, narrow, ring, raw, normed, gain, segment, target, total, keys, values, mask, spread, collect,
    out_wide, in_wide, out_narrow, in_narrow, slots_out, slots_in,
    local_sem, g_send, g_recv, z_send, z_recv, a_send, a_recv, s_sem, word,
):
    dp, fsdp = lax.axis_index("dp"), lax.axis_index("fsdp")
    z, core = dp // 2, lax.rem(dp, 2)
    y, x = fsdp // 4, lax.rem(fsdp, 4)
    other = 1 - core
    x_up, x_down, x_far = lax.rem(x + 1, 4), lax.rem(x + 3, 4), lax.rem(x + 2, 4)
    y_up, y_down, y_far = lax.rem(y + 1, 4), lax.rem(y + 3, 4), lax.rem(y + 2, 4)
    to_x_up, to_x_down = (dp, y * 4 + x_up), (dp, y * 4 + x_down)
    to_y_up, to_y_down = (dp, y_up * 4 + x), (dp, y_down * 4 + x)
    to_z_up = (lax.rem(z + 1, 8) * 2 + core, fsdp)
    to_z_down = (lax.rem(z + 7, 8) * 2 + core, fsdp)
    sibling = (dp + other - core, fsdp)
    to_x_far, to_y_far = (dp, y * 4 + x_far), (dp, y_far * 4 + x)

    def chunk(j):
        return wide.at[j] if j < 3 else narrow.at[j - 3]

    barrier = pltpu.get_barrier_semaphore()

    def here(peer):
        pl.semaphore_signal(barrier, inc=1, device_id=peer, device_id_type=MESH)

    for peer in (to_x_up, to_x_down, to_y_up, to_y_down, to_x_far, to_y_far, sibling):
        here(peer)
    pl.when(z < 7)(lambda: here(to_z_up))
    pl.when(z == 0)(lambda: here(to_z_down))

    def entry():
        pl.semaphore_wait(barrier, 7 + (z + 7) // 8 + z // 7)

        def answer(peer):
            pl.semaphore_signal(word.at[4], inc=1, device_id=peer, device_id_type=MESH)

        pl.when(z > 0)(lambda: answer(to_z_down))
        pl.when(z == 7)(lambda: answer(to_z_up))

    def answers():
        pl.when(z < 7)(lambda: pl.semaphore_wait(word.at[4], 2 - (z + 7) // 8))

    def tell(n):
        for peer in (to_z_up, to_z_down):
            pl.semaphore_signal(word.at[n], inc=1, device_id=peer, device_id_type=MESH)

    def hear(n):
        pl.semaphore_wait(word.at[n], 2)

    ring_half, ring_part = z // 4, lax.rem(z, 4)
    u, v = (1 - ring_half) * y + ring_half * x, (1 - ring_half) * x + ring_half * y
    own_ring = pltpu.make_async_copy(
        weight.at[core, ring_half, ring_part, :, :, pl.ds(*RING)],
        ring.at[ring_half, core, u, v, ring_part],
        local_sem.at[2],
    )
    own_ring.start()
    for j, (start, width) in enumerate(CHUNKS):
        for half, (line, place) in enumerate(((y, x), (x, y))):
            pltpu.make_async_copy(
                weight.at[core, half, :, :, :, pl.ds(start, width)],
                chunk(j).at[half, core, line, place],
                local_sem.at[3],
            ).start()

    loads = [
        pltpu.make_async_copy(source, landing, sem)
        for source, landing, sem in (
            (target_in, target, local_sem.at[0]),
            (segment_in, segment, local_sem.at[1]),
            (gain_in, gain, local_sem.at[4]),
            (hidden, raw, local_sem.at[5]),
        )
    ]
    for copy in loads:
        copy.start()

    def send(view, device, send_sem, recv_sem):
        pltpu.make_async_remote_copy(
            src_ref=view, dst_ref=view, send_sem=send_sem, recv_sem=recv_sem,
            device_id=device, device_id_type=MESH,
        ).start()

    def landed(view, sem):
        pltpu.make_async_copy(view, view, sem).wait()

    low, high = pl.ds(0, 2), pl.ds(2, 2)

    def own_blocks():
        own_ring.wait()
        landed(raw.at[pl.ds(0, 32), pl.ds(0, FEATURES)], local_sem.at[3])

    def near(j):
        g, s, r = chunk(j), g_send.at[j], g_recv.at[j, NEAR]
        send(g.at[0, core, y, x], to_x_up, s, r)
        send(g.at[0, core, y, x], to_x_down, s, r)
        send(g.at[1, core, x, y], to_y_up, s, r)
        send(g.at[1, core, x, y], to_y_down, s, r)
        if j in DIRECT:
            send(g.at[0, core, y, x], (dp, y * 4 + x_far), s, r)
            send(g.at[1, core, x, y], (dp, y_far * 4 + x), s, r)

    def far(j):
        g, s, r = chunk(j), g_send.at[j], g_recv.at[j, FAR]
        landed(g.at[0, core, y], g_recv.at[j, NEAR])
        send(g.at[0, core, y, x_down, low], to_x_up, s, r)
        send(g.at[0, core, y, x_up, high], to_x_down, s, r)
        send(g.at[1, core, x, y_down, low], to_y_up, s, r)
        send(g.at[1, core, x, y_up, high], to_y_down, s, r)

    def lines(j):
        g, s, r, t = chunk(j), g_send.at[j], g_recv.at[j, LINE], g_recv.at[j, TWIN]
        if j in DIRECT:
            landed(g.at[0, core, pl.ds(0, 2), pl.ds(0, 3)], g_recv.at[j, NEAR])
        else:
            landed(g.at[0, core, y, low], g_recv.at[j, FAR])
        send(g.at[0, core, y], to_y_up, s, r)
        send(g.at[0, core, y], to_y_down, s, r)
        send(g.at[1, core, x], to_x_up, s, r)
        send(g.at[1, core, x], to_x_down, s, r)
        send(g.at[0, core, y], sibling, s, t)
        send(g.at[1, core, x], sibling, s, t)

    def pass_lines(j):
        g, s, r, t = chunk(j), g_send.at[j], g_recv.at[j, LAST], g_recv.at[j, TWIN]
        landed(g.at[0, core], g_recv.at[j, LINE])
        send(g.at[0, core, y_down, low], to_y_up, s, r)
        send(g.at[0, core, y_up, high], to_y_down, s, r)
        send(g.at[1, core, x_down, low], to_x_up, s, r)
        send(g.at[1, core, x_up, high], to_x_down, s, r)
        send(g.at[0, core, y_down], sibling, s, t)
        send(g.at[0, core, y_up], sibling, s, t)
        send(g.at[1, core, x_down], sibling, s, t)
        send(g.at[1, core, x_up], sibling, s, t)

    def last_lines(j):
        g, s, t = chunk(j), g_send.at[j], g_recv.at[j, TWIN_LAST]
        landed(g.at[0, core, low], g_recv.at[j, LAST])
        send(g.at[0, core, y_far], sibling, s, t)
        send(g.at[1, core, x_far], sibling, s, t)

    def twin(j):
        landed(chunk(j).at[:, other, pl.ds(0, 3)], g_recv.at[j, TWIN])

    def twin_last(j):
        landed(chunk(j).at[:, other, 0], g_recv.at[j, TWIN_LAST])

    def ring_at(where, h):
        return ring.at[where // 4, core, :, :, lax.rem(where, 4), h]

    def z_up(n):
        return lax.rem(z + n, 8)

    def z_down(n):
        return lax.rem(z + 8 - n, 8)

    def beside(k, along):
        u_to, v_to = lax.rem(u + k * (1 - along), 4), lax.rem(v + k * along, 4)
        return (dp, (1 - ring_half) * (u_to * 4 + v_to) + ring_half * (v_to * 4 + u_to))

    def plane(h):
        for k in (1, 3, 2):
            view = ring.at[ring_half, core, u, v, ring_part, h]
            send(view, beside(k, 1 - h), z_send.at[0], z_recv.at[10 + h])

    def plane_lines(h):
        view = ring.at[ring_half, core, u, pl.ds(0, 3), ring_part, h]
        landed(view, z_recv.at[10 + h])
        if h == 0:
            view = ring.at[ring_half, core, u, :, ring_part, h]
        else:
            view = ring.at[ring_half, core, :, v, ring_part, h]
        for k in (1, 3, 2):
            send(view, beside(k, h), z_send.at[0], z_recv.at[1 + h])

    def to_sibling(where, h):
        send(ring_at(where, h), sibling, z_send.at[1], z_recv.at[0])

    def ring_start(h):
        landed(ring.at[ring_half, core, pl.ds(0, 3), :, ring_part, h], z_recv.at[1 + h])
        send(ring_at(z, h), to_z_up, z_send.at[1], z_recv.at[3 + h])
        send(ring_at(z, h), to_z_down, z_send.at[1], z_recv.at[3 + h])
        to_sibling(z, h)

    def ring_step(n, h):
        landed(ring.at[ring_half, core, :, :, ring_part], z_recv.at[2 * n + 1 + h])
        sem = z_recv.at[2 * n + 3 + h] if n < 3 else z_recv.at[9]
        if n < 3 or h == 0:
            send(ring_at(z_down(n), h), to_z_up, z_send.at[1], sem)
        if n < 3 or h == 1:
            send(ring_at(z_up(n), h), to_z_down, z_send.at[1], sem)
        to_sibling(z_down(n), h)
        to_sibling(z_up(n), h)

    def ring_end():
        landed(ring.at[ring_half, core, :, :, ring_part], z_recv.at[9])
        to_sibling(z_up(4), 0)
        to_sibling(z_up(4), 1)

    def ring_twin():
        landed(ring.at[:, other], z_recv.at[0])

    def plan():
        loads[0].wait()
        loads[1].wait()
        goal = target[...]
        shard, slot = goal >> 12, goal & (ROWS - 1)
        chosen = lax.broadcasted_iota(jnp.int32, (PEERS, ROWS), 0) == shard
        onehot = chosen.astype(jnp.float32)
        earlier = (
            lax.broadcasted_iota(jnp.int32, (ROWS, ROWS), 0)
            < lax.broadcasted_iota(jnp.int32, (ROWS, ROWS), 1)
        ).astype(jnp.bfloat16)
        before = nn(onehot.astype(jnp.bfloat16), earlier)
        rank = jnp.sum(onehot * before, axis=0, keepdims=True).astype(jnp.int32)
        bucket = shard * CAPACITY + rank
        spread[...] = (
            lax.broadcasted_iota(jnp.int32, (PEERS * CAPACITY, ROWS), 0) == bucket
        ).astype(jnp.bfloat16)
        lane = rank + CAPACITY * lax.rem(dp, 4)
        place = (lax.broadcasted_iota(jnp.int32, (128, ROWS), 0) == lane).astype(jnp.bfloat16)
        marks = (onehot * (slot + 1).astype(jnp.float32)).astype(jnp.bfloat16)
        table = nt(marks, place)
        slots_out[...] = jnp.broadcast_to(table[:, None, :], (PEERS, 8, 128))
        ids = jnp.broadcast_to(segment[...].astype(jnp.float32), (ROWS, ROWS))
        causal = lax.broadcasted_iota(jnp.int32, (ROWS, ROWS), 1) <= lax.broadcasted_iota(
            jnp.int32, (ROWS, ROWS), 0
        )
        mask[...] = ((ids == ids.T) & causal).astype(jnp.float32)

    def to_peers(source, landing, send_sem, recv_sem):
        def ship(peer):
            pltpu.make_async_remote_copy(
                src_ref=source.at[peer], dst_ref=landing.at[dp],
                send_sem=send_sem, recv_sem=recv_sem,
                device_id=(peer, fsdp), device_id_type=MESH,
            ).start()

        def ship_two(k, carry):
            ship(lax.rem(dp + 8 + k, PEERS))
            ship(lax.rem(dp + 8 - k, PEERS))
            return carry

        ship(lax.rem(dp + 8, PEERS))
        lax.fori_loop(1, 8, ship_two, 0)
        landing[dp] = source[dp]

    def from_peers(landing, recv_sem):
        landed(landing.at[pl.ds(0, PEERS - 1)], recv_sem)

    def plan_arrivals():
        from_peers(slots_in, s_sem.at[1])
        wanted = lax.broadcasted_iota(jnp.int32, (ROWS, 128), 0) + 1
        for t in range(4):
            row = slots_in[4 * t] + slots_in[4 * t + 1] + slots_in[4 * t + 2] + slots_in[4 * t + 3]
            row = row[0:1].astype(jnp.int32)
            collect[:, t * 128 : (t + 1) * 128] = (wanted == row).astype(jnp.bfloat16)

    def normalise(part):
        if part == 0:
            loads[2].wait()
            loads[3].wait()

        def some(i, carry):
            rows = pl.ds(pl.multiple_of(i * 16, 16), 16)
            floats = raw[rows, :].astype(jnp.float32)
            scale = lax.rsqrt(jnp.mean(floats * floats, axis=1, keepdims=True) + EPS)
            for shard in range(16):
                for c in range(2):
                    for half in range(2):
                        a = shard * 512 + c * 256 + half * 128
                        at = (1 - half) * shard + half * (shard % 4 * 4 + shard // 4)
                        b = ((half * 2 + c) * 16 + at) * 128
                        part = raw[rows, a : a + 128].astype(jnp.float32)
                        normed[rows, b : b + 128] = (part * scale * gain[:, a : a + 128]).astype(
                            jnp.bfloat16
                        )
            return carry

        lax.fori_loop(part * 8, part * 8 + 8, some, 0)

    def project_ring():
        total[5] = jnp.zeros((ROWS, 256), jnp.float32)

        def some(i, carry):
            columns = pl.ds(pl.multiple_of(i * 2048, 2048), 2048)
            block = ring[i // 2, lax.rem(i, 2)].reshape(2048, 256)
            total[5] += nn(normed[:, columns], block)
            return carry

        lax.fori_loop(0, 4, some, 0)

    def project_lines(j, c, mine):
        g, width = chunk(j), CHUNKS[j][1]
        sums = None
        for half in range(2):
            for line in mine[half]:
                first = ((half * 2 + c) * 16 + line * 4) * 128
                columns = pl.ds(pl.multiple_of(first, 512), 512)
                part = nn(normed[:, columns], g[half, c, line].reshape(512, width))
                sums = part if sums is None else sums + part
        return sums

    near_lines, far_lines = ((y, y_up, y_down), (x, x_up, x_down)), ((y_far,), (x_far,))

    def project_own(j):
        total[j, :, : CHUNKS[j][1]] = project_lines(j, core, near_lines)

    def project_twin(j):
        twin(j)
        total[j, :, : CHUNKS[j][1]] += project_lines(j, other, near_lines)

    def project_last(j):
        sums = project_lines(j, core, far_lines)
        twin_last(j)
        total[j, :, : CHUNKS[j][1]] += sums + project_lines(j, other, far_lines)

    def keep():
        keys[...] = total[0, :, :HEAD].astype(jnp.bfloat16)
        values[...] = total[0, :, HEAD:].astype(jnp.bfloat16)

    def group(n):
        if n == 5:
            return out_wide.at[2], in_wide.at[2], 256, RING[0]
        if n < 3:
            return out_wide.at[n - 1], in_wide.at[n - 1], 256, CHUNKS[n][0]
        return out_narrow.at[n - 3], in_narrow.at[n - 3], 128, CHUNKS[n][0]

    def attend(n):
        outgoing, incoming, width, start = group(n)
        contexts = []
        for h in range(width // HEAD):
            query = total[n, :, h * HEAD : (h + 1) * HEAD].astype(jnp.bfloat16)
            scores = nt(query, keys[...]) * HEAD ** (-0.5)
            scores = jnp.where(mask[...] > 0.5, scores, -1e30)
            expos = jnp.exp(scores - jnp.max(scores, axis=1, keepdims=True))
            weights = (expos * (1.0 / jnp.sum(expos, axis=1, keepdims=True))).astype(jnp.bfloat16)
            contexts.append(nn(weights, values[...]).astype(jnp.bfloat16))
        context = jnp.concatenate(contexts, axis=1) if len(contexts) > 1 else contexts[0]
        outgoing[...] = nn(spread[...], context).astype(jnp.bfloat16).reshape(PEERS, CAPACITY, width)
        to_peers(outgoing, incoming, a_send.at[0], a_recv.at[n - 1])

    def deliver(n):
        outgoing, incoming, width, start = group(n)
        from_peers(incoming, a_recv.at[n - 1])
        rows = incoming[...].reshape(PEERS * CAPACITY, width)
        out[:, start : start + width] = nn(collect[...], rows).astype(jnp.bfloat16)

    entry()
    own_blocks()
    plane(0)
    plane(1)
    near(0)
    near(1)
    plan()
    normalise(0)
    plane_lines(0)
    plane_lines(1)
    near(2)
    normalise(1)
    lines(0)
    answers()
    tell(0)
    lines(1)
    ring_start(0)
    ring_start(1)
    far(2)
    hear(0)
    tell(1)
    ring_step(1, 0)
    pass_lines(0)
    ring_step(1, 1)
    project_own(0)
    hear(1)
    tell(2)
    project_twin(0)
    ring_step(2, 0)
    pass_lines(1)
    lines(2)
    near(3)
    near(4)
    ring_step(2, 1)
    project_own(1)
    hear(2)
    tell(3)
    last_lines(0)
    project_last(0)
    keep()
    ring_step(3, 0)
    project_twin(1)
    ring_step(3, 1)
    last_lines(1)
    project_last(1)
    hear(3)
    to_peers(slots_out, slots_in, s_sem.at[0], s_sem.at[1])
    attend(1)
    ring_end()
    pass_lines(2)
    ring_twin()
    project_ring()
    lines(3)
    lines(4)
    attend(5)
    plan_arrivals()
    project_own(2)
    project_twin(2)
    last_lines(2)
    pass_lines(3)
    project_last(2)
    attend(2)
    project_own(3)
    pass_lines(4)
    project_twin(3)
    last_lines(3)
    project_own(4)
    project_twin(4)
    project_last(3)
    attend(3)
    last_lines(4)
    project_last(4)
    attend(4)
    deliver(1)
    deliver(5)
    deliver(2)
    deliver(3)
    deliver(4)
    for j, (start, width) in enumerate(CHUNKS):
        landed(raw.at[pl.ds(0, width), pl.ds(0, 7936)], g_send.at[j])
    landed(raw.at[pl.ds(0, 16), pl.ds(0, 7680)], z_send.at[0])
    landed(raw.at[pl.ds(0, 240)], z_send.at[1])
    landed(slots_out.at[pl.ds(0, PEERS - 1)], s_sem.at[0])
    landed(raw.at[pl.ds(0, 64), pl.ds(0, 7680)], a_send.at[0])

def per_device(hidden, gain, qkv_weight, owner_segment, target_row):
    any_space = pl.BlockSpec(memory_space=pl.ANY)
    vmem = pl.BlockSpec(memory_space=pltpu.VMEM)
    bf16, f32 = jnp.bfloat16, jnp.float32
    dma = pltpu.SemaphoreType.DMA
    return pl.pallas_call(
        kernel,
        out_shape=pltpu.VMEM((ROWS, COLUMNS), bf16),
        in_specs=[any_space] * 5,
        out_specs=vmem,
        scratch_shapes=[
            pltpu.VMEM((3, 2, 2, 4, 4, 4, 2, 16, 256), bf16),
            pltpu.VMEM((2, 2, 2, 4, 4, 4, 2, 16, 128), bf16),
            pltpu.VMEM((2, 2, 4, 4, 4, 2, 16, 256), bf16),
            pltpu.VMEM((ROWS, FEATURES), bf16),
            pltpu.VMEM((ROWS, FEATURES), bf16),
            pltpu.VMEM((1, FEATURES), f32),
            pltpu.VMEM((1, ROWS), jnp.int32),
            pltpu.VMEM((1, ROWS), jnp.int32),
            pltpu.VMEM((6, ROWS, 256), f32),
            pltpu.VMEM((ROWS, HEAD), bf16),
            pltpu.VMEM((ROWS, HEAD), bf16),
            pltpu.VMEM((ROWS, ROWS), f32),
            pltpu.VMEM((PEERS * CAPACITY, ROWS), bf16),
            pltpu.VMEM((ROWS, PEERS * CAPACITY), bf16),
            pltpu.VMEM((3, PEERS, CAPACITY, 256), bf16),
            pltpu.VMEM((3, PEERS, CAPACITY, 256), bf16),
            pltpu.VMEM((2, PEERS, CAPACITY, 128), bf16),
            pltpu.VMEM((2, PEERS, CAPACITY, 128), bf16),
            pltpu.VMEM((PEERS, 8, 128), f32),
            pltpu.VMEM((PEERS, 8, 128), f32),
            dma((6,)),
            dma((len(CHUNKS),)),
            dma((len(CHUNKS), 6)),
            dma((2,)),
            dma((12,)),
            dma((1,)),
            dma((5,)),
            dma((2,)),
            pltpu.SemaphoreType.REGULAR((5,)),
        ],
        compiler_params=pltpu.CompilerParams(
            collective_id=0, has_side_effects=True, vmem_limit_bytes=56 << 20
        ),
        cost_estimate=pl.CostEstimate(
            flops=2 * ROWS * FEATURES * 1280, bytes_accessed=6 << 20, transcendentals=8 * ROWS * ROWS
        ),
    )(
        hidden,
        gain.reshape(1, FEATURES),
        qkv_weight.reshape(2, 2, 4, 2, 16, 1280),
        owner_segment.reshape(1, ROWS),
        target_row.reshape(1, ROWS),
    )


def solution(mesh):
    in_specs = (P(("dp", "fsdp"), None), P(), P("fsdp", None), P(("dp", "fsdp")), P(("dp", "fsdp")))
    out_specs = P(("dp", "fsdp"), None)
    return jax.shard_map(
        per_device, mesh=mesh, in_specs=in_specs, out_specs=out_specs, check_vma=False
    )
```

```python
import jax
import jax.numpy as jnp
from jax import lax
from jax.experimental import pallas as pl
from jax.experimental.pallas import tpu as pltpu
from jax.sharding import PartitionSpec as P

MESH = pl.DeviceIdType.MESH
HEAD = 128
EPS = 1e-05
ROWS = 256
FEATURES = 8192
PEERS = 16
CAPACITY = 32
CHUNKS = ((1024, 256), (0, 256), (512, 256), (768, 128), (896, 128))
RING = (256, 256)
COLUMNS = 1024
DIRECT = (0, 1, 3, 4)
NEAR, FAR, LINE, LAST, TWIN, TWIN_LAST = range(6)


def nt(a, b):
    return lax.dot_general(a, b, (((1,), (1,)), ((), ())), preferred_element_type=jnp.float32)


def nn(a, b):
    return jnp.dot(a, b, preferred_element_type=jnp.float32)


def kernel(
    hidden, gain_in, weight, segment_in, target_in, out,
    wide, narrow, ring, raw, normed, gain, segment, target, total, keys, values, mask, spread, collect,
    out_wide, in_wide, out_narrow, in_narrow, slots_out, slots_in,
    local_sem, g_send, g_recv, z_send, z_recv, a_send, a_recv, s_sem, word,
):
    dp, fsdp = lax.axis_index("dp"), lax.axis_index("fsdp")
    z, core = dp // 2, lax.rem(dp, 2)
    y, x = fsdp // 4, lax.rem(fsdp, 4)
    other = 1 - core
    x_up, x_down, x_far = lax.rem(x + 1, 4), lax.rem(x + 3, 4), lax.rem(x + 2, 4)
    y_up, y_down, y_far = lax.rem(y + 1, 4), lax.rem(y + 3, 4), lax.rem(y + 2, 4)
    to_x_up, to_x_down = (dp, y * 4 + x_up), (dp, y * 4 + x_down)
    to_y_up, to_y_down = (dp, y_up * 4 + x), (dp, y_down * 4 + x)
    to_z_up = (lax.rem(z + 1, 8) * 2 + core, fsdp)
    to_z_down = (lax.rem(z + 7, 8) * 2 + core, fsdp)
    sibling = (dp + other - core, fsdp)
    to_x_far, to_y_far = (dp, y * 4 + x_far), (dp, y_far * 4 + x)

    def chunk(j):
        return wide.at[j] if j < 3 else narrow.at[j - 3]

    barrier = pltpu.get_barrier_semaphore()

    def here(peer):
        pl.semaphore_signal(barrier, inc=1, device_id=peer, device_id_type=MESH)

    for peer in (to_x_up, to_x_down, to_y_up, to_y_down, to_x_far, to_y_far, sibling):
        here(peer)
    pl.when(z < 7)(lambda: here(to_z_up))
    pl.when(z == 0)(lambda: here(to_z_down))

    def entry():
        pl.semaphore_wait(barrier, 7 + (z + 7) // 8 + z // 7)

        def answer(peer):
            pl.semaphore_signal(word.at[4], inc=1, device_id=peer, device_id_type=MESH)

        pl.when(z > 0)(lambda: answer(to_z_down))
        pl.when(z == 7)(lambda: answer(to_z_up))

    def answers():
        pl.when(z < 7)(lambda: pl.semaphore_wait(word.at[4], 2 - (z + 7) // 8))

    def tell(n):
        for peer in (to_z_up, to_z_down):
            pl.semaphore_signal(word.at[n], inc=1, device_id=peer, device_id_type=MESH)

    def hear(n):
        pl.semaphore_wait(word.at[n], 2)

    ring_half, ring_part = z // 4, lax.rem(z, 4)
    u, v = (1 - ring_half) * y + ring_half * x, (1 - ring_half) * x + ring_half * y
    own_ring = pltpu.make_async_copy(
        weight.at[core, ring_half, ring_part, :, :, pl.ds(*RING)],
        ring.at[ring_half, core, u, v, ring_part],
        local_sem.at[2],
    )
    own_ring.start()
    for j, (start, width) in enumerate(CHUNKS):
        for half, (line, place) in enumerate(((y, x), (x, y))):
            pltpu.make_async_copy(
                weight.at[core, half, :, :, :, pl.ds(start, width)],
                chunk(j).at[half, core, line, place],
                local_sem.at[3],
            ).start()

    loads = [
        pltpu.make_async_copy(source, landing, sem)
        for source, landing, sem in (
            (target_in, target, local_sem.at[0]),
            (segment_in, segment, local_sem.at[1]),
            (gain_in, gain, local_sem.at[4]),
            (hidden, raw, local_sem.at[5]),
        )
    ]
    for copy in loads:
        copy.start()

    def send(view, device, send_sem, recv_sem):
        pltpu.make_async_remote_copy(
            src_ref=view, dst_ref=view, send_sem=send_sem, recv_sem=recv_sem,
            device_id=device, device_id_type=MESH,
        ).start()

    def landed(view, sem):
        pltpu.make_async_copy(view, view, sem).wait()

    low, high = pl.ds(0, 2), pl.ds(2, 2)

    def own_blocks():
        own_ring.wait()
        landed(raw.at[pl.ds(0, 32), pl.ds(0, FEATURES)], local_sem.at[3])

    def near(j):
        g, s, r = chunk(j), g_send.at[j], g_recv.at[j, NEAR]
        send(g.at[0, core, y, x], to_x_up, s, r)
        send(g.at[0, core, y, x], to_x_down, s, r)
        send(g.at[1, core, x, y], to_y_up, s, r)
        send(g.at[1, core, x, y], to_y_down, s, r)
        if j in DIRECT:
            send(g.at[0, core, y, x], (dp, y * 4 + x_far), s, r)
            send(g.at[1, core, x, y], (dp, y_far * 4 + x), s, r)

    def far(j):
        g, s, r = chunk(j), g_send.at[j], g_recv.at[j, FAR]
        landed(g.at[0, core, y], g_recv.at[j, NEAR])
        send(g.at[0, core, y, x_down, low], to_x_up, s, r)
        send(g.at[0, core, y, x_up, high], to_x_down, s, r)
        send(g.at[1, core, x, y_down, low], to_y_up, s, r)
        send(g.at[1, core, x, y_up, high], to_y_down, s, r)

    def lines(j):
        g, s, r, t = chunk(j), g_send.at[j], g_recv.at[j, LINE], g_recv.at[j, TWIN]
        if j in DIRECT:
            landed(g.at[0, core, pl.ds(0, 2), pl.ds(0, 3)], g_recv.at[j, NEAR])
        else:
            landed(g.at[0, core, y, low], g_recv.at[j, FAR])
        send(g.at[0, core, y], to_y_up, s, r)
        send(g.at[0, core, y], to_y_down, s, r)
        send(g.at[1, core, x], to_x_up, s, r)
        send(g.at[1, core, x], to_x_down, s, r)
        send(g.at[0, core, y], sibling, s, t)
        send(g.at[1, core, x], sibling, s, t)

    def pass_lines(j):
        g, s, r, t = chunk(j), g_send.at[j], g_recv.at[j, LAST], g_recv.at[j, TWIN]
        landed(g.at[0, core], g_recv.at[j, LINE])
        send(g.at[0, core, y_down, low], to_y_up, s, r)
        send(g.at[0, core, y_up, high], to_y_down, s, r)
        send(g.at[1, core, x_down, low], to_x_up, s, r)
        send(g.at[1, core, x_up, high], to_x_down, s, r)
        send(g.at[0, core, y_down], sibling, s, t)
        send(g.at[0, core, y_up], sibling, s, t)
        send(g.at[1, core, x_down], sibling, s, t)
        send(g.at[1, core, x_up], sibling, s, t)

    def last_lines(j):
        g, s, t = chunk(j), g_send.at[j], g_recv.at[j, TWIN_LAST]
        landed(g.at[0, core, low], g_recv.at[j, LAST])
        send(g.at[0, core, y_far], sibling, s, t)
        send(g.at[1, core, x_far], sibling, s, t)

    def twin(j):
        landed(chunk(j).at[:, other, pl.ds(0, 3)], g_recv.at[j, TWIN])

    def twin_last(j):
        landed(chunk(j).at[:, other, 0], g_recv.at[j, TWIN_LAST])

    def ring_at(where, h):
        return ring.at[where // 4, core, :, :, lax.rem(where, 4), h]

    def z_up(n):
        return lax.rem(z + n, 8)

    def z_down(n):
        return lax.rem(z + 8 - n, 8)

    def beside(k, along):
        u_to, v_to = lax.rem(u + k * (1 - along), 4), lax.rem(v + k * along, 4)
        return (dp, (1 - ring_half) * (u_to * 4 + v_to) + ring_half * (v_to * 4 + u_to))

    def plane(h):
        for k in (1, 3, 2):
            view = ring.at[ring_half, core, u, v, ring_part, h]
            send(view, beside(k, 1 - h), z_send.at[0], z_recv.at[10 + h])

    def plane_lines(h):
        view = ring.at[ring_half, core, u, pl.ds(0, 3), ring_part, h]
        landed(view, z_recv.at[10 + h])
        if h == 0:
            view = ring.at[ring_half, core, u, :, ring_part, h]
        else:
            view = ring.at[ring_half, core, :, v, ring_part, h]
        for k in (1, 3, 2):
            send(view, beside(k, h), z_send.at[0], z_recv.at[1 + h])

    def to_sibling(where, h):
        send(ring_at(where, h), sibling, z_send.at[1], z_recv.at[0])

    def ring_start(h):
        landed(ring.at[ring_half, core, pl.ds(0, 3), :, ring_part, h], z_recv.at[1 + h])
        send(ring_at(z, h), to_z_up, z_send.at[1], z_recv.at[3 + h])
        send(ring_at(z, h), to_z_down, z_send.at[1], z_recv.at[3 + h])
        to_sibling(z, h)

    def ring_step(n, h):
        landed(ring.at[ring_half, core, :, :, ring_part], z_recv.at[2 * n + 1 + h])
        sem = z_recv.at[2 * n + 3 + h] if n < 3 else z_recv.at[9]
        if n < 3 or h == 0:
            send(ring_at(z_down(n), h), to_z_up, z_send.at[1], sem)
        if n < 3 or h == 1:
            send(ring_at(z_up(n), h), to_z_down, z_send.at[1], sem)
        to_sibling(z_down(n), h)
        to_sibling(z_up(n), h)

    def ring_end():
        landed(ring.at[ring_half, core, :, :, ring_part], z_recv.at[9])
        to_sibling(z_up(4), 0)
        to_sibling(z_up(4), 1)

    def ring_twin():
        landed(ring.at[:, other], z_recv.at[0])

    def plan():
        loads[0].wait()
        loads[1].wait()
        goal = target[...]
        shard, slot = goal >> 12, goal & (ROWS - 1)
        chosen = lax.broadcasted_iota(jnp.int32, (PEERS, ROWS), 0) == shard
        onehot = chosen.astype(jnp.float32)
        earlier = (
            lax.broadcasted_iota(jnp.int32, (ROWS, ROWS), 0)
            < lax.broadcasted_iota(jnp.int32, (ROWS, ROWS), 1)
        ).astype(jnp.bfloat16)
        before = nn(onehot.astype(jnp.bfloat16), earlier)
        rank = jnp.sum(onehot * before, axis=0, keepdims=True).astype(jnp.int32)
        bucket = shard * CAPACITY + rank
        spread[...] = (
            lax.broadcasted_iota(jnp.int32, (PEERS * CAPACITY, ROWS), 0) == bucket
        ).astype(jnp.bfloat16)
        lane = rank + CAPACITY * lax.rem(dp, 4)
        place = (lax.broadcasted_iota(jnp.int32, (128, ROWS), 0) == lane).astype(jnp.bfloat16)
        marks = (onehot * (slot + 1).astype(jnp.float32)).astype(jnp.bfloat16)
        table = nt(marks, place)
        slots_out[...] = jnp.broadcast_to(table[:, None, :], (PEERS, 8, 128))
        ids = jnp.broadcast_to(segment[...].astype(jnp.float32), (ROWS, ROWS))
        causal = lax.broadcasted_iota(jnp.int32, (ROWS, ROWS), 1) <= lax.broadcasted_iota(
            jnp.int32, (ROWS, ROWS), 0
        )
        mask[...] = ((ids == ids.T) & causal).astype(jnp.float32)

    def to_peers(source, landing, send_sem, recv_sem):
        def ship(peer):
            pltpu.make_async_remote_copy(
                src_ref=source.at[peer], dst_ref=landing.at[dp],
                send_sem=send_sem, recv_sem=recv_sem,
                device_id=(peer, fsdp), device_id_type=MESH,
            ).start()

        def ship_two(k, carry):
            ship(lax.rem(dp + 8 + k, PEERS))
            ship(lax.rem(dp + 8 - k, PEERS))
            return carry

        ship(lax.rem(dp + 8, PEERS))
        lax.fori_loop(1, 8, ship_two, 0)
        landing[dp] = source[dp]

    def from_peers(landing, recv_sem):
        landed(landing.at[pl.ds(0, PEERS - 1)], recv_sem)

    def plan_arrivals():
        from_peers(slots_in, s_sem.at[1])
        wanted = lax.broadcasted_iota(jnp.int32, (ROWS, 128), 0) + 1
        for t in range(4):
            row = slots_in[4 * t] + slots_in[4 * t + 1] + slots_in[4 * t + 2] + slots_in[4 * t + 3]
            row = row[0:1].astype(jnp.int32)
            collect[:, t * 128 : (t + 1) * 128] = (wanted == row).astype(jnp.bfloat16)

    def normalise(part):
        if part == 0:
            loads[2].wait()
            loads[3].wait()

        def some(i, carry):
            rows = pl.ds(pl.multiple_of(i * 16, 16), 16)
            floats = raw[rows, :].astype(jnp.float32)
            scale = lax.rsqrt(jnp.mean(floats * floats, axis=1, keepdims=True) + EPS)
            for shard in range(16):
                for c in range(2):
                    for half in range(2):
                        a = shard * 512 + c * 256 + half * 128
                        at = (1 - half) * shard + half * (shard % 4 * 4 + shard // 4)
                        b = ((half * 2 + c) * 16 + at) * 128
                        part = raw[rows, a : a + 128].astype(jnp.float32)
                        normed[rows, b : b + 128] = (part * scale * gain[:, a : a + 128]).astype(
                            jnp.bfloat16
                        )
            return carry

        lax.fori_loop(part * 8, part * 8 + 8, some, 0)

    def project_ring():
        total[5] = jnp.zeros((ROWS, 256), jnp.float32)

        def some(i, carry):
            columns = pl.ds(pl.multiple_of(i * 2048, 2048), 2048)
            block = ring[i // 2, lax.rem(i, 2)].reshape(2048, 256)
            total[5] += nn(normed[:, columns], block)
            return carry

        lax.fori_loop(0, 4, some, 0)

    def project_lines(j, c, mine):
        g, width = chunk(j), CHUNKS[j][1]
        sums = None
        for half in range(2):
            for line in mine[half]:
                first = ((half * 2 + c) * 16 + line * 4) * 128
                columns = pl.ds(pl.multiple_of(first, 512), 512)
                part = nn(normed[:, columns], g[half, c, line].reshape(512, width))
                sums = part if sums is None else sums + part
        return sums

    near_lines, far_lines = ((y, y_up, y_down), (x, x_up, x_down)), ((y_far,), (x_far,))

    def project_own(j):
        total[j, :, : CHUNKS[j][1]] = project_lines(j, core, near_lines)

    def project_twin(j):
        twin(j)
        total[j, :, : CHUNKS[j][1]] += project_lines(j, other, near_lines)

    def project_last(j):
        sums = project_lines(j, core, far_lines)
        twin_last(j)
        total[j, :, : CHUNKS[j][1]] += sums + project_lines(j, other, far_lines)

    def keep():
        keys[...] = total[0, :, :HEAD].astype(jnp.bfloat16)
        values[...] = total[0, :, HEAD:].astype(jnp.bfloat16)

    def group(n):
        if n == 5:
            return out_wide.at[2], in_wide.at[2], 256, RING[0]
        if n < 3:
            return out_wide.at[n - 1], in_wide.at[n - 1], 256, CHUNKS[n][0]
        return out_narrow.at[n - 3], in_narrow.at[n - 3], 128, CHUNKS[n][0]

    def attend(n):
        outgoing, incoming, width, start = group(n)
        contexts = []
        for h in range(width // HEAD):
            query = total[n, :, h * HEAD : (h + 1) * HEAD].astype(jnp.bfloat16)
            scores = nt(query, keys[...]) * HEAD ** (-0.5)
            scores = jnp.where(mask[...] > 0.5, scores, -1e30)
            expos = jnp.exp(scores - jnp.max(scores, axis=1, keepdims=True))
            weights = (expos * (1.0 / jnp.sum(expos, axis=1, keepdims=True))).astype(jnp.bfloat16)
            contexts.append(nn(weights, values[...]).astype(jnp.bfloat16))
        context = jnp.concatenate(contexts, axis=1) if len(contexts) > 1 else contexts[0]
        outgoing[...] = nn(spread[...], context).astype(jnp.bfloat16).reshape(PEERS, CAPACITY, width)
        to_peers(outgoing, incoming, a_send.at[0], a_recv.at[n - 1])

    def deliver(n):
        outgoing, incoming, width, start = group(n)
        from_peers(incoming, a_recv.at[n - 1])
        rows = incoming[...].reshape(PEERS * CAPACITY, width)
        out[:, start : start + width] = nn(collect[...], rows).astype(jnp.bfloat16)

    entry()
    own_blocks()
    plane(0)
    plane(1)
    near(0)
    near(1)
    plan()
    normalise(0)
    plane_lines(0)
    plane_lines(1)
    near(2)
    normalise(1)
    lines(0)
    answers()
    tell(0)
    lines(1)
    ring_start(0)
    ring_start(1)
    far(2)
    hear(0)
    tell(1)
    ring_step(1, 0)
    pass_lines(0)
    ring_step(1, 1)
    project_own(0)
    hear(1)
    tell(2)
    project_twin(0)
    ring_step(2, 0)
    pass_lines(1)
    lines(2)
    near(3)
    near(4)
    ring_step(2, 1)
    project_own(1)
    hear(2)
    tell(3)
    last_lines(0)
    project_last(0)
    keep()
    ring_step(3, 0)
    project_twin(1)
    ring_step(3, 1)
    last_lines(1)
    project_last(1)
    hear(3)
    to_peers(slots_out, slots_in, s_sem.at[0], s_sem.at[1])
    attend(1)
    ring_end()
    pass_lines(2)
    ring_twin()
    lines(3)
    project_ring()
    lines(4)
    attend(5)
    plan_arrivals()
    project_own(2)
    project_twin(2)
    last_lines(2)
    pass_lines(3)
    project_last(2)
    attend(2)
    project_own(3)
    pass_lines(4)
    project_twin(3)
    last_lines(3)
    project_own(4)
    project_twin(4)
    project_last(3)
    attend(3)
    last_lines(4)
    project_last(4)
    attend(4)
    deliver(1)
    deliver(5)
    deliver(2)
    deliver(3)
    deliver(4)
    for j, (start, width) in enumerate(CHUNKS):
        landed(raw.at[pl.ds(0, width), pl.ds(0, 7936)], g_send.at[j])
    landed(raw.at[pl.ds(0, 16), pl.ds(0, 7680)], z_send.at[0])
    landed(raw.at[pl.ds(0, 240)], z_send.at[1])
    landed(slots_out.at[pl.ds(0, PEERS - 1)], s_sem.at[0])
    landed(raw.at[pl.ds(0, 64), pl.ds(0, 7680)], a_send.at[0])

def per_device(hidden, gain, qkv_weight, owner_segment, target_row):
    any_space = pl.BlockSpec(memory_space=pl.ANY)
    vmem = pl.BlockSpec(memory_space=pltpu.VMEM)
    bf16, f32 = jnp.bfloat16, jnp.float32
    dma = pltpu.SemaphoreType.DMA
    return pl.pallas_call(
        kernel,
        out_shape=pltpu.VMEM((ROWS, COLUMNS), bf16),
        in_specs=[any_space] * 5,
        out_specs=vmem,
        scratch_shapes=[
            pltpu.VMEM((3, 2, 2, 4, 4, 4, 2, 16, 256), bf16),
            pltpu.VMEM((2, 2, 2, 4, 4, 4, 2, 16, 128), bf16),
            pltpu.VMEM((2, 2, 4, 4, 4, 2, 16, 256), bf16),
            pltpu.VMEM((ROWS, FEATURES), bf16),
            pltpu.VMEM((ROWS, FEATURES), bf16),
            pltpu.VMEM((1, FEATURES), f32),
            pltpu.VMEM((1, ROWS), jnp.int32),
            pltpu.VMEM((1, ROWS), jnp.int32),
            pltpu.VMEM((6, ROWS, 256), f32),
            pltpu.VMEM((ROWS, HEAD), bf16),
            pltpu.VMEM((ROWS, HEAD), bf16),
            pltpu.VMEM((ROWS, ROWS), f32),
            pltpu.VMEM((PEERS * CAPACITY, ROWS), bf16),
            pltpu.VMEM((ROWS, PEERS * CAPACITY), bf16),
            pltpu.VMEM((3, PEERS, CAPACITY, 256), bf16),
            pltpu.VMEM((3, PEERS, CAPACITY, 256), bf16),
            pltpu.VMEM((2, PEERS, CAPACITY, 128), bf16),
            pltpu.VMEM((2, PEERS, CAPACITY, 128), bf16),
            pltpu.VMEM((PEERS, 8, 128), f32),
            pltpu.VMEM((PEERS, 8, 128), f32),
            dma((6,)),
            dma((len(CHUNKS),)),
            dma((len(CHUNKS), 6)),
            dma((2,)),
            dma((12,)),
            dma((1,)),
            dma((5,)),
            dma((2,)),
            pltpu.SemaphoreType.REGULAR((5,)),
        ],
        compiler_params=pltpu.CompilerParams(
            collective_id=0, has_side_effects=True, vmem_limit_bytes=56 << 20
        ),
        cost_estimate=pl.CostEstimate(
            flops=2 * ROWS * FEATURES * 1280, bytes_accessed=6 << 20, transcendentals=8 * ROWS * ROWS
        ),
    )(
        hidden,
        gain.reshape(1, FEATURES),
        qkv_weight.reshape(2, 2, 4, 2, 16, 1280),
        owner_segment.reshape(1, ROWS),
        target_row.reshape(1, ROWS),
    )


def solution(mesh):
    in_specs = (P(("dp", "fsdp"), None), P(), P("fsdp", None), P(("dp", "fsdp")), P(("dp", "fsdp")))
    out_specs = P(("dp", "fsdp"), None)
    return jax.shard_map(
        per_device, mesh=mesh, in_specs=in_specs, out_specs=out_specs, check_vma=False
    )
```
